256 devices in a mesh: section: 16 (over x_hi, y, core), dp: 16 (over z, x_lo).
Axes of the slice: x: 4 (x_hi: 2, x_lo: 2; x = x_hi * 2 + x_lo), y: 4, z: 8, core: 2. Of those that a mesh axis runs over, the one named last changes fastest.
Arguments:
- handed: bfloat16 [16, 2048, 4096], P('section', 'dp'), may hold values from -6 to 6
- lengths: int32 [16, 16, 4], P('section', 'dp'), may hold values from 1 to 64, as said below
- placement: int32 [16, 4, 2], replicated, may hold values from 0 to 3, as said below
- frozen: bfloat16 [16, 4096, 4096], P('section', None, 'dp'), may hold values from -0.09375 to 0.09375
- adapter_down_weight: bfloat16 [16, 4, 64, 4096], P('section'), may hold values from -0.09375 to 0.09375
- adapter_up_weight: bfloat16 [16, 4, 64, 4096], P('section'), may hold values from -0.75 to 0.75
- cotangent: bfloat16 [16, 2048, 4096], P('section', 'dp'), may hold values from -0.29882812 to 0.29882812
Outputs:
- passed: bfloat16 [16, 2048, 4096], P('section', 'dp')
- grad_a: float32 [16, 4, 64, 4096], P('section', None, None, 'dp')
- grad_b: float32 [16, 4, 64, 4096], P('section', None, None, 'dp')
The draws below stay inside these ranges and needn't reach their ends.
Inputs may be any that keep to these rules, and one draw needn't show every extreme that they name: placement[s, j] = (o, k) names slot k of section s + o - 1 as the host of job j's adapter at section s's layer; o is 1 for all jobs but at most one with o = 2 (host: the next section) and at most one with o = 0 (host: the previous section), never past the first or last section; every slot of every section hosts exactly one adapter. Each block's lengths sum to 128, each at least 1. In every section below the last some block has 64 rows of the job whose adapter the next section hosts; in every section above the first some block has 64 rows of the job whose adapter the previous section hosts.
All inputs are finite; a program needn't handle non-finite values.
Results may differ from the reference program's by a relative error of at most 0.0053.
Values may be sent and summed in bfloat16 or wider, within the bound.
No kernel may reach another device: no remote copies, remote signals or barrier semaphores. Data moves between devices by JAX's collectives and lax.ppermute only.
A program may use at most 128 MiB of HBM per device.

```python
import jax
import jax.numpy as jnp
from jax import lax

WINDOW_WIDTH = 4096
ADAPTER_RANK = 64
ADJUST_JOBS = 4
TOK_DEV = 128
MOST = 64
REPLICAS = 16
RELAY_SECTIONS = 16
TOKENS = 2048


def offload_jobs(key):
    section_keys = jax.random.split(key, RELAY_SECTIONS)
    orders = jax.vmap(lambda one_key: jax.random.permutation(one_key, ADJUST_JOBS))(section_keys)
    return (orders[:, 0].astype(jnp.int32), orders[:, 1].astype(jnp.int32))


def draw_placement(key, part):
    up_job, down_job = offload_jobs(key)
    section_ids = jnp.arange(RELAY_SECTIONS, dtype=jnp.int32)[:, None]
    job_ids = jnp.arange(ADJUST_JOBS, dtype=jnp.int32)[None, :]
    final = RELAY_SECTIONS - 1
    sends_up = (job_ids == up_job[:, None]) & (section_ids < final)
    sends_down = (job_ids == down_job[:, None]) & (section_ids > 0)
    offset_code = 1 + sends_up.astype(jnp.int32) - sends_down.astype(jnp.int32)
    up_next = jnp.roll(up_job, -1)
    down_prev = jnp.roll(down_job, 1)
    slot_up = jnp.where(section_ids[:, 0] + 1 < final, up_next, down_job[final])
    slot_down = jnp.where(section_ids[:, 0] - 1 >= 1, down_prev, up_job[0])
    slots = jnp.where(sends_up, slot_up[:, None], jnp.where(sends_down, slot_down[:, None], job_ids))
    return jnp.stack([offset_code, slots], axis=-1).astype(jnp.int32)


def draw_lengths(key, part):
    up_job, down_job = offload_jobs(key)
    key = jax.random.fold_in(key, 23)
    key_pick, key_cut = jax.random.split(key)
    section_ids = jnp.arange(RELAY_SECTIONS, dtype=jnp.int32)[:, None]
    block_ids = jnp.arange(REPLICAS, dtype=jnp.int32)[None, :]
    final = RELAY_SECTIONS - 1
    random_job = jax.random.randint(key_pick, (RELAY_SECTIONS, REPLICAS), 0, ADJUST_JOBS)
    forced = jnp.where((block_ids == 0) & (section_ids < final), up_job[:, None], jnp.where((block_ids == 1) & (section_ids > 0), down_job[:, None], random_job))
    remain = TOK_DEV - MOST
    cut_keys = jax.random.split(key_cut, RELAY_SECTIONS * REPLICAS)

    def pieces_of(one_key):
        picks = jax.random.permutation(one_key, remain - 1)[:ADJUST_JOBS - 2].astype(jnp.int32) + 1
        edges = jnp.concatenate([jnp.zeros((1,), jnp.int32), jnp.sort(picks), jnp.full((1,), remain, jnp.int32)])
        return edges[1:] - edges[:-1]
    pieces = jax.vmap(pieces_of)(cut_keys).reshape(RELAY_SECTIONS, REPLICAS, ADJUST_JOBS - 1)
    job_ids = jnp.arange(ADJUST_JOBS, dtype=jnp.int32)[None, None, :]
    order_ids = job_ids - (job_ids > forced[:, :, None]).astype(jnp.int32)
    picked = jnp.take_along_axis(pieces, jnp.clip(order_ids, 0, ADJUST_JOBS - 2), axis=2)
    return jnp.where(job_ids == forced[:, :, None], MOST, picked).astype(jnp.int32)


def strengthened(array, own_key, source, target, shards_of, factor):
    owner, partner = [(jnp.arange(array.shape[position]) // (array.shape[position] // shards_of)).reshape([-1 if axis == position else 1 for axis in range(array.ndim)]) for position in (source, target)]
    chosen = jax.random.permutation(own_key, shards_of)[partner]
    strong = (owner == chosen) | (owner == (partner + shards_of // 2) % shards_of)
    return jnp.where(strong, factor * array, array)


def shard_levels(stream_key, dims, shards, least, high):
    loudness, own = 1.0, jax.random.fold_in(stream_key, 6)
    for axis_at, parts in shards:
        heights = jnp.exp(jax.random.uniform(jax.random.fold_in(own, axis_at), (parts,), jnp.float32, least / len(shards), high / len(shards)))
        loudness = loudness * jnp.repeat(heights, dims[axis_at] // parts).reshape([-1 if axis == axis_at else 1 for axis in range(len(dims))])
    return loudness


def centred(stream_key, extent, scale, limit, cuts=(), held_as=jnp.bfloat16):
    entries = scale * jax.random.normal(stream_key, extent, jnp.float32)
    if cuts:
        entries = entries * shard_levels(stream_key, extent, cuts, -0.22, 0.18)
    return jnp.clip(entries, -limit, limit).astype(held_as)


def bell_draw_with(stream_key, shape, spread, bound, cuts, heavy, held_as=jnp.bfloat16):
    result = spread * jax.random.normal(stream_key, shape, jnp.float32)
    if cuts:
        result = result * shard_levels(stream_key, shape, cuts, -0.22, 0.18)
    return jnp.clip(strengthened(result, jax.random.fold_in(stream_key, 3), *heavy), -bound, bound).astype(held_as)


def setup_inputs(seed: int = 0) -> dict:
    keys = jax.random.split(jax.random.key(seed), 8)
    return {
        "handed": bell_draw_with(keys[0], (RELAY_SECTIONS, TOKENS, WINDOW_WIDTH), 1.0, 6.0, ((0, 16), (1, 16)), (1, 2, 16, 2.0)),
        "lengths": draw_lengths(jax.random.fold_in(keys[7], 71), 0),
        "placement": draw_placement(jax.random.fold_in(keys[7], 71), 0),
        "frozen": centred(keys[3], (RELAY_SECTIONS, WINDOW_WIDTH, WINDOW_WIDTH), WINDOW_WIDTH ** -0.5, 0.09375, ((0, 16), (2, 16))),
        "adapter_down_weight": centred(keys[4], (RELAY_SECTIONS, ADJUST_JOBS, ADAPTER_RANK, WINDOW_WIDTH), WINDOW_WIDTH ** -0.5, 0.09375, ((0, 16),)),
        "adapter_up_weight": centred(keys[5], (RELAY_SECTIONS, ADJUST_JOBS, ADAPTER_RANK, WINDOW_WIDTH), ADAPTER_RANK ** -0.5, 0.75, ((0, 16),)),
        "cotangent": bell_draw_with(keys[6], (RELAY_SECTIONS, TOKENS, WINDOW_WIDTH), 0.05, 0.29882812, ((0, 16), (1, 16)), (1, 2, 16, 2.0)),
    }


ADAPTER_SCALE = 0.5


def slot_columns(slot_ids, keep_rows):
    column_slot = jnp.arange(ADJUST_JOBS * ADAPTER_RANK, dtype=jnp.int32) // ADAPTER_RANK
    return ((slot_ids[:, None] == column_slot[None, :]) & keep_rows[:, None]).astype(jnp.float32)


def reference(handed, lengths, placement, frozen, adapter_down_weight, adapter_up_weight, cotangent):
    positions = jnp.arange(TOK_DEV, dtype=jnp.int32)
    row_contraction = (((0,), (0,)), ((), ()))
    feature_contraction = (((1,), (1,)), ((), ()))

    def one_section(running, section_id):
        grad_down, grad_up = running
        incoming = lax.dynamic_index_in_dim(handed, (section_id + RELAY_SECTIONS - 1) % RELAY_SECTIONS, 0, keepdims=False)
        upstream_gradient = lax.dynamic_index_in_dim(cotangent, section_id, 0, keepdims=False)
        weight = lax.dynamic_index_in_dim(frozen, section_id, 0, keepdims=False)
        base_out = lax.optimization_barrier(jnp.dot(incoming, weight, preferred_element_type=jnp.float32).astype(jnp.bfloat16))
        counts = lax.dynamic_index_in_dim(lengths, section_id, 0, keepdims=False)
        row_ends = jnp.cumsum(counts, axis=1)
        job_ids = jnp.sum((positions[None, :, None] >= row_ends[:, None, :]).astype(jnp.int32), axis=2).reshape(-1)
        section_plan = lax.dynamic_index_in_dim(placement, section_id, 0, keepdims=False)
        host_section = section_id + jnp.take(section_plan[:, 0], job_ids) - 1
        slot_ids = jnp.take(section_plan[:, 1], job_ids)
        adapted_output = jnp.zeros((TOKENS, WINDOW_WIDTH), jnp.float32)
        for neighbour in (-1, 0, 1):
            target_output = jnp.clip(section_id + neighbour, 0, RELAY_SECTIONS - 1)
            joined_down_maps = lax.dynamic_index_in_dim(adapter_down_weight, target_output, 0, keepdims=False).reshape(ADJUST_JOBS * ADAPTER_RANK, WINDOW_WIDTH)
            joined_up_maps = lax.dynamic_index_in_dim(adapter_up_weight, target_output, 0, keepdims=False).reshape(ADJUST_JOBS * ADAPTER_RANK, WINDOW_WIDTH)
            chosen_slots = slot_columns(slot_ids, host_section == section_id + neighbour)
            rank_codes = (lax.dot_general(incoming, joined_down_maps, feature_contraction, preferred_element_type=jnp.float32) * chosen_slots).astype(jnp.bfloat16)
            adapted_output = adapted_output + ADAPTER_SCALE * jnp.dot(rank_codes, joined_up_maps, preferred_element_type=jnp.float32)
            gradient_signals = (ADAPTER_SCALE * lax.dot_general(upstream_gradient, joined_up_maps, feature_contraction, preferred_element_type=jnp.float32) * chosen_slots).astype(jnp.bfloat16)
            term_down = lax.dot_general(gradient_signals, incoming, row_contraction, preferred_element_type=jnp.float32)
            up_projection_term = ADAPTER_SCALE * lax.dot_general(rank_codes, upstream_gradient, row_contraction, preferred_element_type=jnp.float32)
            grad_down = grad_down.at[target_output].add(term_down.reshape(ADJUST_JOBS, ADAPTER_RANK, WINDOW_WIDTH))
            grad_up = grad_up.at[target_output].add(up_projection_term.reshape(ADJUST_JOBS, ADAPTER_RANK, WINDOW_WIDTH))
        adapted_output = lax.optimization_barrier(adapted_output.astype(jnp.bfloat16))
        passed = (base_out.astype(jnp.float32) + adapted_output.astype(jnp.float32)).astype(jnp.bfloat16)
        return (grad_down, grad_up), passed

    initial = (jnp.zeros((RELAY_SECTIONS, ADJUST_JOBS, ADAPTER_RANK, WINDOW_WIDTH), jnp.float32), jnp.zeros((RELAY_SECTIONS, ADJUST_JOBS, ADAPTER_RANK, WINDOW_WIDTH), jnp.float32))
    (grad_down, grad_up), passed = lax.scan(one_section, initial, jnp.arange(RELAY_SECTIONS, dtype=jnp.int32))
    return passed, grad_down, grad_up
```

```python
import jax
import jax.numpy as jnp
from jax import lax
from jax.sharding import PartitionSpec as P

RANK = 64
JOBS = 4
SCALE = 0.5
LINES = 2
ROWS_BY_ROWS = (((0,), (0,)), ((), ()))
FEATURES = (((1,), (1,)), ((), ()))


def dot32(a, b, dims=(((1,), (0,)), ((), ()))):
    return lax.dot_general(a, b, dims, preferred_element_type=jnp.float32)


def along_z(value, by, depth):
    route = [(z * LINES + x, ((z + by) % depth) * LINES + x) for z in range(depth) for x in range(LINES)]
    return lax.ppermute(value, "dp", route)


def across_x(value, devices):
    return lax.ppermute(value, "dp", [(d, d ^ 1) for d in range(devices)])


def section_shift(value, by, sections):
    route = [(i, i + by) for i in range(sections) if 0 <= i + by < sections]
    return lax.ppermute(value, "section", route)


def hosted_slot(placement, section, code):
    plan = lax.dynamic_index_in_dim(placement, section, 0, keepdims=False)
    return jnp.sum(jnp.where(plan[:, 0] == code, plan[:, 1], 0))


def on_device(handed, lengths, placement, frozen, down, up, cotangent):
    sections = lax.axis_size("section")
    devices = lax.axis_size("dp")
    depth = devices // LINES
    s = lax.axis_index("section")
    d = lax.axis_index("dp")
    z, x = d // LINES, d % LINES
    lines = [[k * LINES + i for k in range(depth)] for i in range(LINES)]
    rows, width = handed.shape[1:]
    half = rows // 2
    cols = width // devices
    wide = width // depth

    ring = [(i, (i + 1) % sections) for i in range(sections)]
    x_a = lax.ppermute(handed[0, :half], "section", ring)
    x_b = lax.ppermute(handed[0, half:], "section", ring)

    for_below = hosted_slot(placement, jnp.maximum(s - 1, 0), 2)
    for_above = hosted_slot(placement, jnp.minimum(s + 1, sections - 1), 0)
    take = lambda w, k: lax.dynamic_index_in_dim(w[0], k, 0, keepdims=False)
    down_above = section_shift(take(down, for_below), -1, sections)
    down_below = section_shift(take(down, for_above), 1, sections)
    up_above = section_shift(take(up, for_below), -1, sections)
    up_below = section_shift(take(up, for_above), 1, sections)
    own_down = down[0].reshape(JOBS * RANK, width)
    own_up = up[0].reshape(JOBS * RANK, width)

    w_own = frozen[0]
    w_pair = across_x(w_own, devices)

    cot = cotangent[0]
    cot_line = lax.all_to_all(
        cot.reshape(rows, depth, wide).swapaxes(0, 1), "dp", 0, 0, axis_index_groups=lines, tiled=True
    ).reshape(depth * rows, wide)

    own = jnp.concatenate([x_a, x_b])
    fwd_a = fwd_b = bwd_a = bwd_b = None
    fwd, bwd = [], []
    pa, pb, qa, qb = x_a, x_b, x_a, x_b
    far = depth // 2
    for _ in range(1, far):
        pa, qa = along_z(pa, 1, depth), along_z(qa, -1, depth)
        pb, qb = along_z(pb, 1, depth), along_z(qb, -1, depth)
        fwd.append((pa, pb))
        bwd.append((qa, qb))
    last = (along_z(pa, 1, depth), along_z(qb, -1, depth))
    blocks = [(x_a, x_b)] + fwd + [last] + bwd[::-1]

    def adapter_of(counts):
        ends = jnp.cumsum(counts, axis=-1)
        job = jnp.sum((jnp.arange(rows, dtype=jnp.int32)[:, None] >= ends[..., None, :]).astype(jnp.int32), axis=-1)
        plan = lax.dynamic_index_in_dim(placement, s, 0, keepdims=False)
        which = jnp.where(plan[:, 0] == 1, plan[:, 1], jnp.where(plan[:, 0] == 2, JOBS, JOBS + 1))
        match = job[..., None] == jnp.arange(JOBS, dtype=jnp.int32)
        return jnp.sum(jnp.where(match, which, 0), axis=-1)

    adapter = adapter_of(lengths[0, 0])
    column = jnp.arange((JOBS + 2) * RANK, dtype=jnp.int32) // RANK
    chosen = adapter[:, None] == column[None, :]

    def masked(own_part, above_part, below_part):
        return jnp.where(chosen, jnp.concatenate([own_part, above_part, below_part], axis=1), 0.0)

    codes = masked(
        dot32(own, own_down, FEATURES), dot32(own, down_above, FEATURES), dot32(own, down_below, FEATURES)
    ).astype(jnp.bfloat16)
    signals = (
        SCALE * masked(dot32(cot, own_up, FEATURES), dot32(cot, up_above, FEATURES), dot32(cot, up_below, FEATURES))
    ).astype(jnp.bfloat16)
    n = JOBS * RANK
    adapted = (
        SCALE
        * (
            dot32(codes[:, :n], own_up)
            + dot32(codes[:, n : n + RANK], up_above)
            + dot32(codes[:, n + RANK :], up_below)
        )
    ).astype(jnp.bfloat16)

    def narrow(v):
        return jnp.sum(v.astype(jnp.float32).reshape(rows, JOBS + 2, RANK), axis=1).astype(jnp.bfloat16)

    tail = jnp.zeros((16, 2 * RANK), jnp.bfloat16).at[0, :JOBS].set(lengths[0, 0].astype(jnp.bfloat16))
    sent = jnp.concatenate([jnp.concatenate([narrow(codes), narrow(signals)], axis=1), tail])
    line = lax.all_gather(sent, "dp", axis_index_groups=lines)
    line_adapter = adapter_of(line[:, rows, :JOBS].astype(jnp.int32))
    line_chosen = line_adapter[:, :, None] == column
    line_codes = jnp.where(line_chosen, jnp.tile(line[:, :rows, :RANK], (1, 1, JOBS + 2)), 0)
    line_signals = jnp.where(line_chosen, jnp.tile(line[:, :rows, RANK:], (1, 1, JOBS + 2)), 0)

    part_up = SCALE * dot32(line_codes.reshape(depth * rows, -1), cot_line, ROWS_BY_ROWS)

    pieces = [None] * depth
    part_down = None
    for k in sorted(range(depth), key=lambda k: min(k, depth - k)):
        block = own if k == 0 else jnp.concatenate(blocks[k])
        piece = jnp.concatenate([dot32(block, w_own), dot32(block, w_pair)], axis=1).astype(jnp.bfloat16)
        pieces[k] = piece if k == 0 else along_z(piece, -k, depth)
        block_signals = lax.dynamic_index_in_dim(line_signals, (z - k) % depth, 0, keepdims=False)
        term = dot32(block_signals, lax.dynamic_slice_in_dim(block, z * wide, wide, 1), ROWS_BY_ROWS)
        part_down = term if part_down is None else part_down + term

    passed = jnp.zeros((rows, width), jnp.bfloat16)
    for k in sorted(range(depth), key=lambda k: min(k, depth - k)):
        for side, piece in ((x, pieces[k][:, :cols]), (1 - x, pieces[k][:, cols:])):
            at = ((z + k) % depth) * wide + side * cols
            added = piece.astype(jnp.float32) + lax.dynamic_slice_in_dim(adapted, at, cols, 1).astype(jnp.float32)
            passed = lax.dynamic_update_slice_in_dim(passed, added.astype(jnp.bfloat16), at, 1)

    slot_below = hosted_slot(placement, jnp.maximum(s - 1, 0), 2)
    slot_above = hosted_slot(placement, jnp.minimum(s + 1, sections - 1), 0)
    slots = jnp.arange(JOBS, dtype=jnp.int32)[:, None, None]

    def gradient(part):
        mine = lax.dynamic_slice_in_dim(part, x * cols, cols, 1)
        theirs = lax.dynamic_slice_in_dim(part, (1 - x) * cols, cols, 1)
        total = (mine + across_x(theirs, devices)).reshape(JOBS + 2, RANK, cols)
        from_below = section_shift(total[JOBS], 1, sections)
        from_above = section_shift(total[JOBS + 1], -1, sections)
        return (
            total[:JOBS]
            + jnp.where(slots == slot_below, from_below[None], 0.0)
            + jnp.where(slots == slot_above, from_above[None], 0.0)
        )[None]

    return passed[None], gradient(part_down), gradient(part_up)


def solution(mesh):
    in_specs = (
        P("section", "dp", None),
        P("section", "dp", None),
        P(),
        P("section", None, "dp"),
        P("section", None, None, None),
        P("section", None, None, None),
        P("section", "dp", None),
    )
    out_specs = (
        P("section", "dp", None),
        P("section", None, None, "dp"),
        P("section", None, None, "dp"),
    )
    return jax.shard_map(on_device, mesh=mesh, in_specs=in_specs, out_specs=out_specs, check_vma=False)
```

```python
import functools

import jax
import jax.numpy as jnp
from jax import lax
from jax.experimental import pallas as pl
from jax.experimental.pallas import tpu as pltpu
from jax.sharding import PartitionSpec as P

RANK = 64
JOBS = 4
SIX = (JOBS + 2) * RANK
SCALE = 0.5
LINES = 2
PAD = 16
FEATURES = (((1,), (1,)), ((), ()))
BF16, F32, I32 = jnp.bfloat16, jnp.float32, jnp.int32


def dot32(a, b):
    return jnp.dot(a, b, preferred_element_type=F32)


def dot_features(a, b):
    return lax.dot_general(a, b, FEATURES, preferred_element_type=F32)


def along_z(value, by, depth):
    route = [(z * LINES + x, ((z + by) % depth) * LINES + x) for z in range(depth) for x in range(LINES)]
    return lax.ppermute(value, "dp", route)


def across_x(value, devices):
    return lax.ppermute(value, "dp", [(d, d ^ 1) for d in range(devices)])


def section_shift(value, by, sections):
    route = [(i, i + by) for i in range(sections) if 0 <= i + by < sections]
    return lax.ppermute(value, "section", route)


def hosted_slot(placement, section, code):
    plan = lax.dynamic_index_in_dim(placement, section, 0, keepdims=False)
    return jnp.sum(jnp.where(plan[:, 0] == code, plan[:, 1], 0))


def in_order(values, *others):
    return lax.optimization_barrier((tuple(values), others))[0]


def kernel_call(kernel, outs, scalars, arrays):
    vmem, smem = pl.BlockSpec(memory_space=pltpu.VMEM), pl.BlockSpec(memory_space=pltpu.SMEM)
    return pl.pallas_call(
        kernel,
        out_shape=tuple(jax.ShapeDtypeStruct(shape, dtype) for shape, dtype in outs),
        in_specs=[smem] * len(scalars) + [vmem] * len(arrays),
        out_specs=tuple(vmem for _ in outs),
        compiler_params=pltpu.CompilerParams(vmem_limit_bytes=40 * 2**20),
        cost_estimate=pl.CostEstimate(flops=1024, bytes_accessed=1024, transcendentals=0),
    )(*scalars, *arrays)


def split_kernel(cot_ref, out_ref):
    wide = out_ref.shape[2]
    for k in range(out_ref.shape[0]):
        out_ref[k] = cot_ref[:, k * wide : (k + 1) * wide]


def iota(shape, dim):
    return lax.broadcasted_iota(I32, shape, dim)


def rows_kernel(place, lengths, plan, xa, xb, cot, own_down, own_up, above, below, adapted, sent):
    rows, width = cot.shape
    first = place[2] * (2 * JOBS)
    which = []
    for j in range(JOBS):
        offset, slot = plan[first + 2 * j], plan[first + 2 * j + 1]
        which.append(jnp.where(offset == 1, slot, jnp.where(offset == 2, JOBS, JOBS + 1)))

    def adapter_of(position):
        found, end = jnp.full(position.shape, which[0], I32), 0
        for j in range(1, JOBS):
            end = end + lengths[j - 1]
            found = jnp.where(position >= end, which[j], found)
        return found

    chosen = adapter_of(iota((rows, SIX), 0)) == lax.shift_right_logical(iota((rows, SIX), 1), 6)
    x = jnp.concatenate([xa[...], xb[...]], axis=0)
    guest_down = jnp.concatenate([above[:RANK], below[:RANK]], axis=0)
    guest_up = jnp.concatenate([above[RANK:], below[RANK:]], axis=0)

    def all_six(v, own, guest):
        return jnp.concatenate([dot_features(v, own[...]), dot_features(v, guest)], axis=1)

    codes = jnp.where(chosen, all_six(x, own_down, guest_down), 0.0).astype(BF16)
    signals = jnp.where(chosen, SCALE * all_six(cot[...], own_up, guest_up), 0.0).astype(BF16)
    own = JOBS * RANK
    tile = width // 8
    for t in range(8):
        at = slice(t * tile, (t + 1) * tile)
        total = dot32(codes[:, :own], own_up[:, at]) + dot32(codes[:, own:], guest_up[:, at])
        adapted[:, at] = (SCALE * total).astype(BF16)
    rank, lane = iota((SIX, 2 * RANK), 0) & (RANK - 1), iota((SIX, 2 * RANK), 1)
    to_codes = (rank == lane).astype(F32).astype(BF16)
    to_signals = (rank + RANK == lane).astype(F32).astype(BF16)
    narrow = (dot32(codes, to_codes) + dot32(signals, to_signals)).astype(BF16)
    ids = adapter_of(iota((PAD, rows), 1)).astype(F32).astype(BF16)
    for k in range(sent.shape[0]):
        sent[k, :rows] = narrow
        sent[k, rows:] = ids


def base_kernel(groups, with_columns, place, *refs):
    blocks, (w_own, w_pair), outs = refs[: 2 * groups], refs[2 * groups : 2 * groups + 2], refs[2 * groups + 2 :]
    half, _ = blocks[0].shape
    rows, cols = 2 * half, w_own.shape[1]
    wide = LINES * cols
    lhs = jnp.concatenate([b[...] for b in blocks], axis=0)
    for w, first in ((w_own, 0), (w_pair, cols)):
        result = dot32(lhs, w[...]).astype(BF16)
        for i in range(groups):
            outs[i][:, first : first + cols] = result[i * rows : (i + 1) * rows]
    if with_columns:
        at = pl.multiple_of(place[0] * wide, wide)
        for i, b in enumerate(blocks):
            outs[groups][i // 2, (i % 2) * half : (i % 2 + 1) * half] = b[:, pl.ds(at, wide)]


def base(place, halves, w_own, w_pair, with_columns=True):
    groups = len(halves) // 2
    half, wide = halves[0].shape[0], LINES * w_own.shape[1]
    outs = [((2 * half, wide), BF16)] * groups
    if with_columns:
        outs = outs + [((groups, 2 * half, wide), BF16)]
    return kernel_call(
        functools.partial(base_kernel, groups, with_columns), outs, [place], [*halves, w_own, w_pair]
    )


def gradient_kernel(of_signals, order, place, line, *refs):
    blocks, (mine, theirs) = refs[:-2], refs[-2:]
    depth, rows = line.shape[0], line.shape[1] - PAD
    cols = mine.shape[1]
    pick = iota((SIX, 2 * RANK), 0) & (RANK - 1)
    pick = (pick + (RANK if of_signals else 0) == iota((SIX, 2 * RANK), 1)).astype(F32).astype(BF16)
    slot = lax.shift_right_logical(iota((SIX, rows), 0), 6)
    lhs = []
    for k in order:
        at = lax.rem(place[0] + (depth - k), depth) if of_signals else k
        spread = dot_features(pick, line[at, :rows])
        ids = line[at, rows : rows + PAD][:1].astype(F32).astype(I32)
        lhs.append(jnp.where(slot == ids, spread, 0.0).astype(BF16))
    values = jnp.concatenate([b[...].reshape(-1, b.shape[-1]) for b in blocks], axis=0)
    total = dot32(jnp.concatenate(lhs, axis=1), values)
    if not of_signals:
        total = SCALE * total
    first = place[1] == 0
    mine[...] = jnp.where(first, total[:, :cols], total[:, cols:])
    theirs[...] = jnp.where(first, total[:, cols:], total[:, :cols]).astype(BF16)


def gradient(of_signals, order, place, line, blocks):
    cols = blocks[0].shape[-1] // LINES
    return kernel_call(
        functools.partial(gradient_kernel, of_signals, order),
        [((SIX, cols), F32), ((SIX, cols), BF16)],
        [place],
        [line, *blocks],
    )


def finish_kernel(depth, cols, place, adapted, *refs):
    pieces, out = refs[:depth], refs[depth]
    z, x = place[0], place[1]
    for k in range(depth):
        for side, first in ((x, 0), (1 - x, cols)):
            at = pl.multiple_of((lax.rem(z + k, depth) * LINES + side) * cols, cols)
            total = pieces[k][:, first : first + cols].astype(F32) + adapted[:, pl.ds(at, cols)].astype(F32)
            out[:, pl.ds(at, cols)] = total.astype(BF16)


def on_device(handed, lengths, placement, frozen, down, up, cotangent):
    sections = lax.axis_size("section")
    devices = lax.axis_size("dp")
    depth = devices // LINES
    far = depth // 2
    s = lax.axis_index("section")
    d = lax.axis_index("dp")
    z, x = d // LINES, d % LINES
    place = jnp.stack([z, x, s]).astype(I32)
    lines = [[k * LINES + i for k in range(depth)] for i in range(LINES)]
    rows, width = handed.shape[1:]
    half = rows // 2
    cols = width // devices
    wide = width // depth
    cot = cotangent[0]

    behind = [(i, (i + 1) % sections) for i in range(sections)]
    xa = lax.ppermute(handed[0, :half], "section", behind)
    xb = lax.ppermute(handed[0, half:], "section", behind)

    def to_line(value):
        return lax.all_to_all(value, "dp", 0, 0, axis_index_groups=lines, tiled=True)

    cot_line = to_line(kernel_call(split_kernel, [((depth, rows, wide), BF16)], [], [cot])[0])

    slot_below = hosted_slot(placement, jnp.maximum(s - 1, 0), 2)
    slot_above = hosted_slot(placement, jnp.minimum(s + 1, sections - 1), 0)
    maps = lambda k: jnp.concatenate([lax.dynamic_index_in_dim(w[0], k, 0, keepdims=False) for w in (down, up)])
    from_above = section_shift(maps(slot_below), -1, sections)
    from_below = section_shift(maps(slot_above), 1, sections)
    own_down = down[0].reshape(JOBS * RANK, width)
    own_up = up[0].reshape(JOBS * RANK, width)

    w_own = frozen[0]
    w_pair = across_x(w_own, devices)

    step = lambda pair: (along_z(pair[0], 1, depth), along_z(pair[1], -1, depth))
    a1 = step((xa, xa))
    b1 = step((xb, xb))
    (xa_,) = in_order((xa,), *a1, cot_line)
    adapted, sent = kernel_call(
        rows_kernel,
        [((rows, width), BF16), ((depth, rows + PAD, 2 * RANK), BF16)],
        [place, lengths.reshape(-1), placement.reshape(-1)],
        [xa_, xb, cot, own_down, own_up, from_above, from_below],
    )
    line = to_line(sent)
    a2 = step(a1)
    b2 = step(b1)
    far_columns = along_z(
        lax.dynamic_slice_in_dim(jnp.concatenate([xa, xb]), ((z + far) % depth) * wide, wide, 1), far, depth
    )
    a3 = step(a2)
    (line_,) = in_order((line,), *b2)
    up_mine, up_theirs = gradient(False, tuple(range(depth)), place, line_, [cot_line])
    up_theirs = across_x(up_theirs, devices)
    b3 = step(b2)

    pieces = [None] * depth
    (xa_,) = in_order((xa,), *a3)
    pieces[0], near_f, near_b, near_columns = base(
        place, (xa_, xb, a1[0], b1[0], a1[1], b1[1]), w_own, w_pair
    )
    pieces[1], pieces[depth - 1] = along_z(near_f, -1, depth), along_z(near_b, 1, depth)
    last_a, last_b = along_z(a3[0], 1, depth), along_z(b3[1], -1, depth)

    f2, r2, f3, r3, next_columns = base(
        place, (a2[0], b2[0], a2[1], b2[1], a3[0], b3[0], a3[1], b3[1]), w_own, w_pair
    )
    pieces[2], pieces[depth - 2] = along_z(f2, -2, depth), along_z(r2, 2, depth)
    pieces[3], pieces[depth - 3] = along_z(f3, -3, depth), along_z(r3, 3, depth)
    order = (0, 1, depth - 1, 2, depth - 2, 3, depth - 3, far)
    down_mine, down_theirs = gradient(True, order, place, line, [near_columns, next_columns, far_columns])
    down_theirs = across_x(down_theirs, devices)

    last_a, last_b = in_order((last_a, last_b), down_mine, up_mine, near_columns, next_columns)
    (last,) = base(place, (last_a, last_b), w_own, w_pair, with_columns=False)
    pieces[far] = along_z(last, far, depth)

    def over_pair(mine, theirs):
        return (mine + theirs.astype(F32)).reshape(JOBS + 2, RANK, cols)

    up_total, down_total = over_pair(up_mine, up_theirs), over_pair(down_mine, down_theirs)
    guests = lambda job: jnp.stack([down_total[job], up_total[job]]).astype(BF16)
    of_below = section_shift(guests(JOBS), 1, sections).astype(F32)
    of_above = section_shift(guests(JOBS + 1), -1, sections).astype(F32)
    slots = jnp.arange(JOBS, dtype=I32)[:, None, None]

    def gathered(total, i):
        return (
            total[:JOBS]
            + jnp.where(slots == slot_below, of_below[i][None], 0.0)
            + jnp.where(slots == slot_above, of_above[i][None], 0.0)
        )[None]

    (passed,) = kernel_call(
        functools.partial(finish_kernel, depth, cols), [((rows, width), BF16)], [place], [adapted, *pieces]
    )
    return passed[None], gathered(down_total, 0), gathered(up_total, 1)


def solution(mesh):
    in_specs = (
        P("section", "dp", None),
        P("section", "dp", None),
        P(),
        P("section", None, "dp"),
        P("section", None, None, None),
        P("section", None, None, None),
        P("section", "dp", None),
    )
    out_specs = (
        P("section", "dp", None),
        P("section", None, None, "dp"),
        P("section", None, None, "dp"),
    )
    return jax.shard_map(on_device, mesh=mesh, in_specs=in_specs, out_specs=out_specs, check_vma=False)
```

```python
import functools

import jax
import jax.numpy as jnp
from jax import lax
from jax.experimental import pallas as pl
from jax.experimental.pallas import tpu as pltpu
from jax.sharding import PartitionSpec as P

RANK = 64
JOBS = 4
SIX = (JOBS + 2) * RANK
SCALE = 0.5
LINES = 2
PAD = 16
FEATURES = (((1,), (1,)), ((), ()))
BF16, F32, I32 = jnp.bfloat16, jnp.float32, jnp.int32


def dot32(a, b):
    return jnp.dot(a, b, preferred_element_type=F32)


def dot_features(a, b):
    return lax.dot_general(a, b, FEATURES, preferred_element_type=F32)


def along_z(value, by, depth):
    route = [(z * LINES + x, ((z + by) % depth) * LINES + x) for z in range(depth) for x in range(LINES)]
    return lax.ppermute(value, "dp", route)


def across_x(value, devices):
    return lax.ppermute(value, "dp", [(d, d ^ 1) for d in range(devices)])


def section_shift(value, by, sections):
    route = [(i, i + by) for i in range(sections) if 0 <= i + by < sections]
    return lax.ppermute(value, "section", route)


def hosted_slot(placement, section, code):
    plan = lax.dynamic_index_in_dim(placement, section, 0, keepdims=False)
    return jnp.sum(jnp.where(plan[:, 0] == code, plan[:, 1], 0))


def in_order(values, *others):
    return lax.optimization_barrier((tuple(values), others))[0]


def kernel_call(kernel, outs, scalars, arrays):
    vmem, smem = pl.BlockSpec(memory_space=pltpu.VMEM), pl.BlockSpec(memory_space=pltpu.SMEM)
    return pl.pallas_call(
        kernel,
        out_shape=tuple(jax.ShapeDtypeStruct(shape, dtype) for shape, dtype in outs),
        in_specs=[smem] * len(scalars) + [vmem] * len(arrays),
        out_specs=tuple(vmem for _ in outs),
        compiler_params=pltpu.CompilerParams(vmem_limit_bytes=40 * 2**20),
        cost_estimate=pl.CostEstimate(flops=1024, bytes_accessed=1024, transcendentals=0),
    )(*scalars, *arrays)


def split_kernel(cot_ref, out_ref):
    wide = out_ref.shape[2]
    for k in range(out_ref.shape[0]):
        out_ref[k] = cot_ref[:, k * wide : (k + 1) * wide]


def iota(shape, dim):
    return lax.broadcasted_iota(I32, shape, dim)


def rows_kernel(place, lengths, plan, own_x, cot, own_down, own_up, above, below, adapted, sent):
    rows, width = cot.shape
    first = place[2] * (2 * JOBS)
    which = []
    for j in range(JOBS):
        offset, slot = plan[first + 2 * j], plan[first + 2 * j + 1]
        which.append(jnp.where(offset == 1, slot, jnp.where(offset == 2, JOBS, JOBS + 1)))

    def adapter_of(position):
        found, end = jnp.full(position.shape, which[0], I32), 0
        for j in range(1, JOBS):
            end = end + lengths[j - 1]
            found = jnp.where(position >= end, which[j], found)
        return found

    chosen = adapter_of(iota((rows, SIX), 0)) == lax.shift_right_logical(iota((rows, SIX), 1), 6)
    x = own_x[...]
    guest_down = jnp.concatenate([above[:RANK], below[:RANK]], axis=0)
    guest_up = jnp.concatenate([above[RANK:], below[RANK:]], axis=0)

    def all_six(v, own, guest):
        return jnp.concatenate([dot_features(v, own[...]), dot_features(v, guest)], axis=1)

    codes = jnp.where(chosen, all_six(x, own_down, guest_down), 0.0).astype(BF16)
    signals = jnp.where(chosen, SCALE * all_six(cot[...], own_up, guest_up), 0.0).astype(BF16)
    own = JOBS * RANK
    tile = width // 8
    for t in range(8):
        at = slice(t * tile, (t + 1) * tile)
        total = dot32(codes[:, :own], own_up[:, at]) + dot32(codes[:, own:], guest_up[:, at])
        adapted[:, at] = (SCALE * total).astype(BF16)
    rank, lane = iota((SIX, 2 * RANK), 0) & (RANK - 1), iota((SIX, 2 * RANK), 1)
    to_codes = (rank == lane).astype(F32).astype(BF16)
    to_signals = (rank + RANK == lane).astype(F32).astype(BF16)
    narrow = (dot32(codes, to_codes) + dot32(signals, to_signals)).astype(BF16)
    ids = adapter_of(iota((PAD, rows), 1)).astype(F32).astype(BF16)
    for k in range(sent.shape[0]):
        sent[k, :rows] = narrow
        sent[k, rows:] = ids


def base_kernel(count, place, *refs):
    blocks, (w_own, w_pair, out, columns) = refs[:count], refs[count:]
    rows, cols = blocks[0].shape[0], w_own.shape[1]
    wide = LINES * cols
    lhs = jnp.concatenate([b[...] for b in blocks], axis=0)
    for w, first in ((w_own, 0), (w_pair, cols)):
        result = dot32(lhs, w[...]).astype(BF16)
        for i in range(count):
            out[i, :, first : first + cols] = result[i * rows : (i + 1) * rows]
    at = pl.multiple_of(place[0] * wide, wide)
    for i, b in enumerate(blocks):
        columns[i] = b[:, pl.ds(at, wide)]


def owners_kernel(order, places, place, done, f3, r3, w_own, w_pair, out, columns):
    rows, cols = f3.shape[0], w_own.shape[1]
    wide = LINES * cols
    owner = lambda k: lax.rem(place[0] + (places - k), places)
    for i, k in enumerate(order[: done.shape[0]]):
        out[owner(k)] = done[i]
    lhs = jnp.concatenate([f3[...], r3[...]], axis=0)
    for w, first in ((w_own, 0), (w_pair, cols)):
        result = dot32(lhs, w[...]).astype(BF16)
        for i, k in enumerate(order[done.shape[0] :]):
            out[owner(k), :, first : first + cols] = result[i * rows : (i + 1) * rows]
    out[owner(places // 2)] = jnp.zeros((rows, wide), BF16)
    at = pl.multiple_of(place[0] * wide, wide)
    for i, b in enumerate((f3, r3)):
        columns[i] = b[:, pl.ds(at, wide)]


def halves_kernel(f3, r3, first, second):
    first[...] = f3[...]
    second[...] = r3[...]


def halves(f3, r3):
    half, width = f3.shape[0] // 2, f3.shape[1]
    tile = width // 4
    shape = jax.ShapeDtypeStruct((half, width), f3.dtype)
    at = lambda i: pl.BlockSpec((half, tile), lambda j: (i, j))
    return pl.pallas_call(
        halves_kernel,
        grid=(width // tile,),
        out_shape=(shape, shape),
        in_specs=[at(0), at(1)],
        out_specs=(at(0), at(0)),
        cost_estimate=pl.CostEstimate(flops=1024, bytes_accessed=1024, transcendentals=0),
    )(f3, r3)


def last_kernel(place, first_half, second_half, w_own, w_pair, out, columns):
    lhs = jnp.concatenate([first_half[...], second_half[...]], axis=0)
    cols = w_own.shape[1]
    for w, first in ((w_own, 0), (w_pair, cols)):
        out[:, first : first + cols] = dot32(lhs, w[...]).astype(BF16)
    at = pl.multiple_of(place[0] * (LINES * cols), LINES * cols)
    half = first_half.shape[0]
    columns[:half] = first_half[:, pl.ds(at, LINES * cols)]
    columns[half:] = second_half[:, pl.ds(at, LINES * cols)]


def gradient_kernel(of_signals, order, place, line, *refs):
    blocks, (mine, theirs) = refs[:-2], refs[-2:]
    depth, rows = line.shape[0], line.shape[1] - PAD
    cols = mine.shape[1]
    pick = iota((SIX, 2 * RANK), 0) & (RANK - 1)
    pick = (pick + (RANK if of_signals else 0) == iota((SIX, 2 * RANK), 1)).astype(F32).astype(BF16)
    slot = lax.shift_right_logical(iota((SIX, rows), 0), 6)
    lhs = []
    for k in order:
        at = lax.rem(place[0] + (depth - k), depth) if of_signals else k
        spread = dot_features(pick, line[at, :rows])
        ids = line[at, rows : rows + PAD][:1].astype(F32).astype(I32)
        lhs.append(jnp.where(slot == ids, spread, 0.0).astype(BF16))
    values = jnp.concatenate([b[...].reshape(-1, b.shape[-1]) for b in blocks], axis=0)
    total = dot32(jnp.concatenate(lhs, axis=1), values)
    if not of_signals:
        total = SCALE * total
    first = place[1] == 0
    mine[...] = jnp.where(first, total[:, :cols], total[:, cols:])
    theirs[...] = jnp.where(first, total[:, cols:], total[:, :cols]).astype(BF16)


def gradient(of_signals, order, place, line, blocks):
    cols = blocks[0].shape[-1] // LINES
    return kernel_call(
        functools.partial(gradient_kernel, of_signals, order),
        [((SIX, cols), F32), ((SIX, cols), BF16)],
        [place],
        [line, *blocks],
    )


def finish_kernel(place, adapted, results, last, out):
    z, x = place[0], place[1]
    depth, cols = results.shape[0], results.shape[2] // LINES

    def add(at_z, piece):
        for side, first in ((x, 0), (1 - x, cols)):
            at = pl.multiple_of((at_z * LINES + side) * cols, cols)
            total = piece[:, first : first + cols].astype(F32) + adapted[:, pl.ds(at, cols)].astype(F32)
            out[:, pl.ds(at, cols)] = total.astype(BF16)

    for k in range(depth):
        add(k, results[k])
    add(lax.rem(z + depth // 2, depth), last[...])


def on_device(handed, lengths, placement, frozen, down, up, cotangent):
    sections = lax.axis_size("section")
    devices = lax.axis_size("dp")
    depth = devices // LINES
    far = depth // 2
    s = lax.axis_index("section")
    d = lax.axis_index("dp")
    z, x = d // LINES, d % LINES
    place = jnp.stack([z, x, s]).astype(I32)
    lines = [[k * LINES + i for k in range(depth)] for i in range(LINES)]
    rows, width = handed.shape[1:]
    half = rows // 2
    cols = width // devices
    wide = width // depth
    cot = cotangent[0]

    own = lax.ppermute(handed[0], "section", [(i, (i + 1) % sections) for i in range(sections)])

    def to_line(value):
        return lax.all_to_all(value, "dp", 0, 0, axis_index_groups=lines, tiled=True)

    cot_line = to_line(kernel_call(split_kernel, [((depth, rows, wide), BF16)], [], [cot])[0])

    step = lambda pair: (along_z(pair[0], 1, depth), along_z(pair[1], -1, depth))
    ring_1 = step((own, own))

    slot_below = hosted_slot(placement, jnp.maximum(s - 1, 0), 2)
    slot_above = hosted_slot(placement, jnp.minimum(s + 1, sections - 1), 0)
    maps = lambda k: jnp.concatenate([lax.dynamic_index_in_dim(w[0], k, 0, keepdims=False) for w in (down, up)])
    to_below, to_above = in_order((maps(slot_below), maps(slot_above)), own)
    from_above = section_shift(to_below, -1, sections)
    from_below = section_shift(to_above, 1, sections)
    own_down = down[0].reshape(JOBS * RANK, width)
    own_up = up[0].reshape(JOBS * RANK, width)

    w_own = frozen[0]
    w_pair = across_x(in_order((w_own,), own)[0], devices)

    ring_2 = step(ring_1)
    (own_,) = in_order((own,), ring_1, cot_line, w_pair)
    adapted, sent = kernel_call(
        rows_kernel,
        [((rows, width), BF16), ((depth, rows + PAD, 2 * RANK), BF16)],
        [place, lengths.reshape(-1), placement.reshape(-1)],
        [own_, cot, own_down, own_up, from_above, from_below],
    )
    line = to_line(sent)

    ring_2 = in_order(ring_2, sent)
    ring_3 = step(ring_2)
    order = (0, 1, depth - 1, 2, depth - 2, 3, depth - 3)
    done, near_columns = kernel_call(
        functools.partial(base_kernel, 5),
        [((5, rows, wide), BF16)] * 2,
        [place],
        [own, *ring_1, *ring_2, w_own, w_pair],
    )

    ring_3 = in_order(ring_3, near_columns)
    half_f, half_r = halves(*ring_3)
    last = along_z(half_f, 1, depth), along_z(half_r, -1, depth)
    ring_3 = in_order(ring_3, half_f)
    results, next_columns = kernel_call(
        functools.partial(owners_kernel, order, depth),
        [((depth, rows, wide), BF16), ((2, rows, wide), BF16)],
        [place],
        [done, *ring_3, w_own, w_pair],
    )
    (line_,) = in_order((line,), results)
    results = to_line(results)
    up_parts = gradient(False, tuple(range(depth)), place, line_, [cot_line])
    last = in_order(last, up_parts)
    last, far_columns = kernel_call(last_kernel, [((rows, wide), BF16)] * 2, [place], [*last, w_own, w_pair])
    result_last = along_z(last, far, depth)
    down_parts = gradient(
        True, order + (far,), place, line, [near_columns, next_columns, far_columns]
    )

    (down_mine, down_theirs), (up_mine, up_theirs) = down_parts, up_parts
    own_rows = JOBS * RANK
    both = lambda v, w, first, last: jnp.stack([v[first:last], w[first:last]]).astype(BF16)
    from_pair = across_x(both(down_theirs, up_theirs, 0, own_rows), devices)

    def to_host(first, by):
        here = both(down_mine, up_mine, first, first + RANK)
        there = both(down_theirs, up_theirs, first, first + RANK)
        moves = [(i, i + by) for i in range(sections) if 0 <= i + by < sections]
        route = [(i * devices + k, j * devices + (k ^ 1)) for i, j in moves for k in range(devices)]
        return section_shift(here, by, sections).astype(F32) + lax.ppermute(
            there, ("section", "dp"), route
        ).astype(F32)

    of_below = to_host(own_rows, 1)
    of_above = to_host(own_rows + RANK, -1)
    slots = jnp.arange(JOBS, dtype=I32)[:, None, None]

    def gathered(mine, i):
        return (
            (mine[:own_rows] + from_pair[i].astype(F32)).reshape(JOBS, RANK, cols)
            + jnp.where(slots == slot_below, of_below[i][None], 0.0)
            + jnp.where(slots == slot_above, of_above[i][None], 0.0)
        )[None]

    (passed,) = kernel_call(
        finish_kernel, [((rows, width), BF16)], [place], [adapted, results, result_last]
    )
    return passed[None], gathered(down_mine, 0), gathered(up_mine, 1)


def solution(mesh):
    in_specs = (
        P("section", "dp", None),
        P("section", "dp", None),
        P(),
        P("section", None, "dp"),
        P("section", None, None, None),
        P("section", None, None, None),
        P("section", "dp", None),
    )
    out_specs = (
        P("section", "dp", None),
        P("section", None, None, "dp"),
        P("section", None, None, "dp"),
    )
    return jax.shard_map(on_device, mesh=mesh, in_specs=in_specs, out_specs=out_specs, check_vma=False)
```

```python
import functools

import jax
import jax.numpy as jnp
from jax import lax
from jax.experimental import pallas as pl
from jax.experimental.pallas import tpu as pltpu
from jax.sharding import PartitionSpec as P

RANK = 64
JOBS = 4
SIX = (JOBS + 2) * RANK
SCALE = 0.5
LINES = 2
PAD = 16
MOVED = 2**20
FEATURES = (((1,), (1,)), ((), ()))
BF16, F32, I32 = jnp.bfloat16, jnp.float32, jnp.int32


def dot32(a, b):
    return jnp.dot(a, b, preferred_element_type=F32)


def dot_features(a, b):
    return lax.dot_general(a, b, FEATURES, preferred_element_type=F32)


def along_z(value, by, depth):
    route = [(z * LINES + x, ((z + by) % depth) * LINES + x) for z in range(depth) for x in range(LINES)]
    return lax.ppermute(value, "dp", route)


def across_x(value, devices):
    return lax.ppermute(value, "dp", [(d, d ^ 1) for d in range(devices)])


def section_shift(value, by, sections):
    route = [(i, i + by) for i in range(sections) if 0 <= i + by < sections]
    return lax.ppermute(value, "section", route)


def hosted_slot(plan, section, code):
    first, slot = section * (2 * JOBS), 0
    for j in range(JOBS):
        slot = slot + jnp.where(plan[first + 2 * j] == code, plan[first + 2 * j + 1], 0)
    return slot


def guest_slots(place, plan):
    s, sections = place[2], plan.shape[0] // (2 * JOBS)
    return (
        hosted_slot(plan, jnp.maximum(s - 1, 0), 2),
        hosted_slot(plan, jnp.minimum(s + 1, sections - 1), 0),
    )


def maps_kernel(place, plan, down, up, to_below, to_above, sems):
    copies = []
    for slot, out in zip(guest_slots(place, plan), (to_below, to_above)):
        for i, maps in enumerate((down, up)):
            copies.append(
                pltpu.make_async_copy(maps.at[slot], out.at[pl.ds(i * RANK, RANK)], sems.at[len(copies)])
            )
    for copy in copies:
        copy.start()
    for copy in copies:
        copy.wait()


def copy_call(kernel, outs, copies, scalars, arrays):
    vmem, smem = pl.BlockSpec(memory_space=pltpu.VMEM), pl.BlockSpec(memory_space=pltpu.SMEM)
    return pl.pallas_call(
        kernel,
        out_shape=tuple(jax.ShapeDtypeStruct(shape, BF16) for shape in outs),
        in_specs=[smem] * len(scalars) + [pl.BlockSpec(memory_space=pl.ANY)] * len(arrays),
        out_specs=tuple(vmem for _ in outs),
        scratch_shapes=[pltpu.SemaphoreType.DMA((copies,))],
        compiler_params=pltpu.CompilerParams(vmem_limit_bytes=40 * 2**20),
        cost_estimate=pl.CostEstimate(flops=1024, bytes_accessed=1024, transcendentals=0),
    )(*scalars, *arrays)


def in_order(values, *others):
    return lax.optimization_barrier((tuple(values), others))[0]


def kernel_call(kernel, outs, scalars, arrays, moved=1024):
    vmem, smem = pl.BlockSpec(memory_space=pltpu.VMEM), pl.BlockSpec(memory_space=pltpu.SMEM)
    return pl.pallas_call(
        kernel,
        out_shape=tuple(jax.ShapeDtypeStruct(shape, dtype) for shape, dtype in outs),
        in_specs=[smem] * len(scalars) + [vmem] * len(arrays),
        out_specs=tuple(vmem for _ in outs),
        compiler_params=pltpu.CompilerParams(vmem_limit_bytes=40 * 2**20),
        cost_estimate=pl.CostEstimate(flops=1024, bytes_accessed=moved, transcendentals=0),
    )(*scalars, *arrays)


def split_kernel(cot_ref, out_ref):
    wide = out_ref.shape[2]
    for k in range(out_ref.shape[0]):
        out_ref[k] = cot_ref[:, k * wide : (k + 1) * wide]


def iota(shape, dim):
    return lax.broadcasted_iota(I32, shape, dim)


def rows_kernel(place, lengths, plan, own_x, cot, own_down, own_up, above, below, adapted, sent):
    rows, width = cot.shape
    first = place[2] * (2 * JOBS)
    which = []
    for j in range(JOBS):
        offset, slot = plan[first + 2 * j], plan[first + 2 * j + 1]
        which.append(jnp.where(offset == 1, slot, jnp.where(offset == 2, JOBS, JOBS + 1)))

    def adapter_of(position):
        found, end = jnp.full(position.shape, which[0], I32), 0
        for j in range(1, JOBS):
            end = end + lengths[j - 1]
            found = jnp.where(position >= end, which[j], found)
        return found

    chosen = adapter_of(iota((rows, SIX), 0)) == lax.shift_right_logical(iota((rows, SIX), 1), 6)
    x = own_x[...]
    guest_down = jnp.concatenate([above[:RANK], below[:RANK]], axis=0)
    guest_up = jnp.concatenate([above[RANK:], below[RANK:]], axis=0)

    def all_six(v, own, guest):
        return jnp.concatenate([dot_features(v, own[...]), dot_features(v, guest)], axis=1)

    codes = jnp.where(chosen, all_six(x, own_down, guest_down), 0.0).astype(BF16)
    signals = jnp.where(chosen, SCALE * all_six(cot[...], own_up, guest_up), 0.0).astype(BF16)
    own = JOBS * RANK
    tile = width // 8
    for t in range(8):
        at = slice(t * tile, (t + 1) * tile)
        total = dot32(codes[:, :own], own_up[:, at]) + dot32(codes[:, own:], guest_up[:, at])
        adapted[:, at] = (SCALE * total).astype(BF16)
    rank, lane = iota((SIX, 2 * RANK), 0) & (RANK - 1), iota((SIX, 2 * RANK), 1)
    to_codes = (rank == lane).astype(F32).astype(BF16)
    to_signals = (rank + RANK == lane).astype(F32).astype(BF16)
    narrow = (dot32(codes, to_codes) + dot32(signals, to_signals)).astype(BF16)
    ids = adapter_of(iota((PAD, rows), 1)).astype(F32).astype(BF16)
    for k in range(sent.shape[0]):
        sent[k, :rows] = narrow
        sent[k, rows:] = ids


def base_kernel(count, place, *refs):
    blocks, (w_own, w_pair, out, columns) = refs[:count], refs[count:]
    rows, cols = blocks[0].shape[0], w_own.shape[1]
    wide = LINES * cols
    lhs = jnp.concatenate([b[...] for b in blocks], axis=0)
    for w, first in ((w_own, 0), (w_pair, cols)):
        result = dot32(lhs, w[...]).astype(BF16)
        for i in range(count):
            out[i, :, first : first + cols] = result[i * rows : (i + 1) * rows]
    at = pl.multiple_of(place[0] * wide, wide)
    for i, b in enumerate(blocks):
        columns[i] = b[:, pl.ds(at, wide)]


def owners_kernel(order, places, place, done, f3, r3, w_own, w_pair, out, columns):
    rows, cols = f3.shape[0], w_own.shape[1]
    wide = LINES * cols
    owner = lambda k: lax.rem(place[0] + (places - k), places)
    for i, k in enumerate(order[: done.shape[0]]):
        out[owner(k)] = done[i]
    lhs = jnp.concatenate([f3[...], r3[...]], axis=0)
    for w, first in ((w_own, 0), (w_pair, cols)):
        result = dot32(lhs, w[...]).astype(BF16)
        for i, k in enumerate(order[done.shape[0] :]):
            out[owner(k), :, first : first + cols] = result[i * rows : (i + 1) * rows]
    out[owner(places // 2)] = jnp.zeros((rows, wide), BF16)
    at = pl.multiple_of(place[0] * wide, wide)
    for i, b in enumerate((f3, r3)):
        columns[i] = b[:, pl.ds(at, wide)]


def halves_kernel(f3, r3, first, second, sems):
    half = first.shape[0]
    copies = (
        pltpu.make_async_copy(f3.at[pl.ds(0, half)], first, sems.at[0]),
        pltpu.make_async_copy(r3.at[pl.ds(half, half)], second, sems.at[1]),
    )
    for copy in copies:
        copy.start()
    for copy in copies:
        copy.wait()


def last_kernel(place, first_half, second_half, w_own, w_pair, out, columns):
    lhs = jnp.concatenate([first_half[...], second_half[...]], axis=0)
    cols = w_own.shape[1]
    for w, first in ((w_own, 0), (w_pair, cols)):
        out[:, first : first + cols] = dot32(lhs, w[...]).astype(BF16)
    at = pl.multiple_of(place[0] * (LINES * cols), LINES * cols)
    half = first_half.shape[0]
    columns[:half] = first_half[:, pl.ds(at, LINES * cols)]
    columns[half:] = second_half[:, pl.ds(at, LINES * cols)]


def gradient_terms(of_signals, order, place, line, blocks):
    depth, rows = line.shape[0], line.shape[1] - PAD
    pick = iota((SIX, 2 * RANK), 0) & (RANK - 1)
    pick = (pick + (RANK if of_signals else 0) == iota((SIX, 2 * RANK), 1)).astype(F32).astype(BF16)
    slot = lax.shift_right_logical(iota((SIX, rows), 0), 6)
    lhs = []
    for k in order:
        at = lax.rem(place[0] + (depth - k), depth) if of_signals else k
        spread = dot_features(pick, line[at, :rows])
        ids = line[at, rows : rows + PAD][:1].astype(F32).astype(I32)
        lhs.append(jnp.where(slot == ids, spread, 0.0).astype(BF16))
    values = jnp.concatenate([b[...].reshape(-1, b.shape[-1]) for b in blocks], axis=0)
    total = dot32(jnp.concatenate(lhs, axis=1), values)
    cols = total.shape[1] // LINES
    left, right = total[:, :cols], total[:, cols:]
    first = place[1] == 0
    return jnp.where(first, left, right), jnp.where(first, right, left)


def up_gradient_kernel(order, place, line, cot_line, mine, theirs):
    here, there = gradient_terms(False, order, place, line, [cot_line])
    mine[...] = SCALE * here
    theirs[...] = (SCALE * there).astype(BF16)


def down_gradient_kernel(order, place, line, *refs):
    blocks, (mine, theirs) = refs[:-2], refs[-2:]
    here, there = gradient_terms(True, order, place, line, blocks)
    mine[...] = here
    theirs[...] = there.astype(BF16)


def finish_kernel(place, adapted, results, last, out):
    z, x = place[0], place[1]
    depth, cols = results.shape[0], results.shape[2] // LINES

    def add(at_z, piece):
        for side, first in ((x, 0), (1 - x, cols)):
            at = pl.multiple_of((at_z * LINES + side) * cols, cols)
            total = piece[:, first : first + cols].astype(F32) + adapted[:, pl.ds(at, cols)].astype(F32)
            out[:, pl.ds(at, cols)] = total.astype(BF16)

    for k in range(depth):
        add(k, results[k])
    add(lax.rem(z + depth // 2, depth), last[...])


def on_device(handed, lengths, placement, frozen, down, up, cotangent):
    sections = lax.axis_size("section")
    devices = lax.axis_size("dp")
    depth = devices // LINES
    far = depth // 2
    s = lax.axis_index("section")
    d = lax.axis_index("dp")
    place = jnp.stack([lax.shift_right_logical(d, 1), d & (LINES - 1), s]).astype(I32)
    plan = placement.reshape(-1)
    lines = [[k * LINES + i for k in range(depth)] for i in range(LINES)]
    rows, width = handed.shape[1:]
    half = rows // 2
    cols = width // devices
    wide = width // depth
    cot = cotangent[0]

    own = lax.ppermute(handed[0], "section", [(i, (i + 1) % sections) for i in range(sections)])

    def to_line(value):
        return lax.all_to_all(value, "dp", 0, 0, axis_index_groups=lines, tiled=True)

    cot_line = to_line(kernel_call(split_kernel, [((depth, rows, wide), BF16)], [], [cot])[0])

    step = lambda pair: (along_z(pair[0], 1, depth), along_z(pair[1], -1, depth))
    ring_1 = step((own, own))

    to_below, to_above = in_order(
        copy_call(maps_kernel, [(2 * RANK, width)] * 2, 4, [place, plan], [down[0], up[0]]), own
    )
    from_above = section_shift(to_below, -1, sections)
    from_below = section_shift(to_above, 1, sections)
    own_down = down[0].reshape(JOBS * RANK, width)
    own_up = up[0].reshape(JOBS * RANK, width)

    w_own = frozen[0]
    w_pair = across_x(in_order((w_own,), to_below)[0], devices)

    ring_1 = in_order(ring_1, cot_line)
    ring_2 = step(ring_1)
    (own_,) = in_order((own,), ring_1, cot_line, w_pair)
    adapted, sent = kernel_call(
        rows_kernel,
        [((rows, width), BF16), ((depth, rows + PAD, 2 * RANK), BF16)],
        [place, lengths.reshape(-1), plan],
        [own_, cot, own_down, own_up, from_above, from_below],
    )
    line = to_line(sent)

    ring_2 = in_order(ring_2, sent)
    ring_3 = step(ring_2)
    order = (0, 1, depth - 1, 2, depth - 2, 3, depth - 3)
    done, near_columns = kernel_call(
        functools.partial(base_kernel, 5),
        [((5, rows, wide), BF16)] * 2,
        [place],
        [own, *ring_1, *ring_2, w_own, w_pair],
    )

    ring_3 = in_order(ring_3, near_columns)
    half_f, half_r = copy_call(halves_kernel, [(half, width)] * 2, 2, [], ring_3)
    last = along_z(half_f, 1, depth), along_z(half_r, -1, depth)
    ring_3 = in_order(ring_3, half_f)
    results, next_columns = kernel_call(
        functools.partial(owners_kernel, order, depth),
        [((depth, rows, wide), BF16), ((2, rows, wide), BF16)],
        [place],
        [done, *ring_3, w_own, w_pair],
    )
    (line_,) = in_order((line,), results)
    results = to_line(results)
    terms = ((SIX, cols), F32)
    up_mine, up_theirs = kernel_call(
        functools.partial(up_gradient_kernel, tuple(range(depth))),
        [terms, ((SIX, cols), BF16)],
        [place],
        [line_, cot_line],
    )
    up_theirs = across_x(up_theirs, devices)
    last = in_order(last, up_mine)
    last, far_columns = kernel_call(last_kernel, [((rows, wide), BF16)] * 2, [place], [*last, w_own, w_pair], MOVED)
    result_last = along_z(last, far, depth)
    down_mine, down_theirs = kernel_call(
        functools.partial(down_gradient_kernel, order + (far,)),
        [terms, ((SIX, cols), BF16)],
        [place],
        [line, near_columns, next_columns, far_columns],
    )
    down_theirs = across_x(down_theirs, devices)

    over_pair = lambda mine, theirs: (mine + theirs.astype(F32)).reshape(JOBS + 2, RANK, cols)
    up_sum, down_sum = over_pair(up_mine, up_theirs), over_pair(down_mine, down_theirs)
    next_rows, prev_rows = (jnp.stack([down_sum[k], up_sum[k]]).astype(BF16) for k in (JOBS, JOBS + 1))
    of_below = section_shift(next_rows, 1, sections).astype(F32)
    of_above = section_shift(prev_rows, -1, sections).astype(F32)
    slots = jnp.arange(JOBS, dtype=I32)[:, None, None]

    def hosted(section, code):
        jobs = lax.dynamic_index_in_dim(placement, section, 0, keepdims=False)
        return jnp.sum(jnp.where(jobs[:, 0] == code, jobs[:, 1], 0))

    slot_below, slot_above = hosted(jnp.maximum(s - 1, 0), 2), hosted(jnp.minimum(s + 1, sections - 1), 0)

    def gathered(mine, i):
        return (
            mine[:JOBS]
            + jnp.where(slots == slot_below, of_below[i][None], 0.0)
            + jnp.where(slots == slot_above, of_above[i][None], 0.0)
        )[None]

    (passed,) = kernel_call(
        finish_kernel, [((rows, width), BF16)], [place], [adapted, results, result_last]
    )
    return passed[None], gathered(down_sum, 0), gathered(up_sum, 1)


def solution(mesh):
    in_specs = (
        P("section", "dp", None),
        P("section", "dp", None),
        P(),
        P("section", None, "dp"),
        P("section", None, None, None),
        P("section", None, None, None),
        P("section", "dp", None),
    )
    out_specs = (
        P("section", "dp", None),
        P("section", None, None, "dp"),
        P("section", None, None, "dp"),
    )
    return jax.shard_map(on_device, mesh=mesh, in_specs=in_specs, out_specs=out_specs, check_vma=False)
```

```python
import functools

import jax
import jax.numpy as jnp
from jax import lax
from jax.experimental import pallas as pl
from jax.experimental.pallas import tpu as pltpu
from jax.sharding import PartitionSpec as P

RANK = 64
JOBS = 4
SIX = (JOBS + 2) * RANK
SCALE = 0.5
LINES = 2
PAD = 16
MOVED = 2**20
FEATURES = (((1,), (1,)), ((), ()))
BF16, F32, I32 = jnp.bfloat16, jnp.float32, jnp.int32


def dot32(a, b):
    return jnp.dot(a, b, preferred_element_type=F32)


def dot_features(a, b):
    return lax.dot_general(a, b, FEATURES, preferred_element_type=F32)


def along_z(value, by, depth):
    route = [(z * LINES + x, ((z + by) % depth) * LINES + x) for z in range(depth) for x in range(LINES)]
    return lax.ppermute(value, "dp", route)


def across_x(value, devices):
    return lax.ppermute(value, "dp", [(d, d ^ 1) for d in range(devices)])


def section_shift(value, by, sections):
    route = [(i, i + by) for i in range(sections) if 0 <= i + by < sections]
    return lax.ppermute(value, "section", route)


def hosted_slot(plan, section, code):
    first, slot = section * (2 * JOBS), 0
    for j in range(JOBS):
        slot = slot + jnp.where(plan[first + 2 * j] == code, plan[first + 2 * j + 1], 0)
    return slot


def guest_slots(place, plan):
    s, sections = place[2], plan.shape[0] // (2 * JOBS)
    return (
        hosted_slot(plan, jnp.maximum(s - 1, 0), 2),
        hosted_slot(plan, jnp.minimum(s + 1, sections - 1), 0),
    )


def maps_kernel(place, plan, down, up, to_below, to_above, sems):
    copies = []
    for slot, out in zip(guest_slots(place, plan), (to_below, to_above)):
        for i, maps in enumerate((down, up)):
            copies.append(
                pltpu.make_async_copy(maps.at[slot], out.at[pl.ds(i * RANK, RANK)], sems.at[len(copies)])
            )
    for copy in copies:
        copy.start()
    for copy in copies:
        copy.wait()


def copy_call(kernel, outs, copies, scalars, arrays):
    vmem, smem = pl.BlockSpec(memory_space=pltpu.VMEM), pl.BlockSpec(memory_space=pltpu.SMEM)
    return pl.pallas_call(
        kernel,
        out_shape=tuple(jax.ShapeDtypeStruct(shape, BF16) for shape in outs),
        in_specs=[smem] * len(scalars) + [pl.BlockSpec(memory_space=pl.ANY)] * len(arrays),
        out_specs=tuple(vmem for _ in outs),
        scratch_shapes=[pltpu.SemaphoreType.DMA((copies,))],
        compiler_params=pltpu.CompilerParams(vmem_limit_bytes=40 * 2**20),
        cost_estimate=pl.CostEstimate(flops=1024, bytes_accessed=1024, transcendentals=0),
    )(*scalars, *arrays)


def in_order(values, *others):
    return lax.optimization_barrier((tuple(values), others))[0]


def kernel_call(kernel, outs, scalars, arrays, moved=1024):
    vmem, smem = pl.BlockSpec(memory_space=pltpu.VMEM), pl.BlockSpec(memory_space=pltpu.SMEM)
    return pl.pallas_call(
        kernel,
        out_shape=tuple(jax.ShapeDtypeStruct(shape, dtype) for shape, dtype in outs),
        in_specs=[smem] * len(scalars) + [vmem] * len(arrays),
        out_specs=tuple(vmem for _ in outs),
        compiler_params=pltpu.CompilerParams(vmem_limit_bytes=40 * 2**20),
        cost_estimate=pl.CostEstimate(flops=1024, bytes_accessed=moved, transcendentals=0),
    )(*scalars, *arrays)


def split_kernel(cot_ref, out_ref):
    wide = out_ref.shape[2]
    for k in range(out_ref.shape[0]):
        out_ref[k] = cot_ref[:, k * wide : (k + 1) * wide]


def iota(shape, dim):
    return lax.broadcasted_iota(I32, shape, dim)


def rows_kernel(place, lengths, plan, own_x, cot, own_down, own_up, above, below, adapted, sent):
    rows, width = cot.shape
    first = place[2] * (2 * JOBS)
    which = []
    for j in range(JOBS):
        offset, slot = plan[first + 2 * j], plan[first + 2 * j + 1]
        which.append(jnp.where(offset == 1, slot, jnp.where(offset == 2, JOBS, JOBS + 1)))

    def adapter_of(position):
        found, end = jnp.full(position.shape, which[0], I32), 0
        for j in range(1, JOBS):
            end = end + lengths[j - 1]
            found = jnp.where(position >= end, which[j], found)
        return found

    chosen = adapter_of(iota((rows, SIX), 0)) == lax.shift_right_logical(iota((rows, SIX), 1), 6)
    x = own_x[...]
    guest_down = jnp.concatenate([above[:RANK], below[:RANK]], axis=0)
    guest_up = jnp.concatenate([above[RANK:], below[RANK:]], axis=0)

    def all_six(v, own, guest):
        return jnp.concatenate([dot_features(v, own[...]), dot_features(v, guest)], axis=1)

    codes = jnp.where(chosen, all_six(x, own_down, guest_down), 0.0).astype(BF16)
    signals = jnp.where(chosen, SCALE * all_six(cot[...], own_up, guest_up), 0.0).astype(BF16)
    own = JOBS * RANK
    tile = width // 8
    for t in range(8):
        at = slice(t * tile, (t + 1) * tile)
        total = dot32(codes[:, :own], own_up[:, at]) + dot32(codes[:, own:], guest_up[:, at])
        adapted[:, at] = (SCALE * total).astype(BF16)
    rank, lane = iota((SIX, 2 * RANK), 0) & (RANK - 1), iota((SIX, 2 * RANK), 1)
    to_codes = (rank == lane).astype(F32).astype(BF16)
    to_signals = (rank + RANK == lane).astype(F32).astype(BF16)
    narrow = (dot32(codes, to_codes) + dot32(signals, to_signals)).astype(BF16)
    ids = adapter_of(iota((PAD, rows), 1)).astype(F32).astype(BF16)
    for k in range(sent.shape[0]):
        sent[k, :rows] = narrow
        sent[k, rows:] = ids


def base_kernel(count, place, *refs):
    blocks, (w_own, w_pair, out, columns) = refs[:count], refs[count:]
    rows, cols = blocks[0].shape[0], w_own.shape[1]
    wide = LINES * cols
    lhs = jnp.concatenate([b[...] for b in blocks], axis=0)
    for w, first in ((w_own, 0), (w_pair, cols)):
        result = dot32(lhs, w[...]).astype(BF16)
        for i in range(count):
            out[i, :, first : first + cols] = result[i * rows : (i + 1) * rows]
    at = pl.multiple_of(place[0] * wide, wide)
    for i, b in enumerate(blocks):
        columns[i] = b[:, pl.ds(at, wide)]


def owners_kernel(order, places, place, done, f3, r3, w_own, w_pair, out, columns):
    rows, cols = f3.shape[0], w_own.shape[1]
    wide = LINES * cols
    owner = lambda k: lax.rem(place[0] + (places - k), places)
    for i, k in enumerate(order[: done.shape[0]]):
        out[owner(k)] = done[i]
    lhs = jnp.concatenate([f3[...], r3[...]], axis=0)
    for w, first in ((w_own, 0), (w_pair, cols)):
        result = dot32(lhs, w[...]).astype(BF16)
        for i, k in enumerate(order[done.shape[0] :]):
            out[owner(k), :, first : first + cols] = result[i * rows : (i + 1) * rows]
    out[owner(places // 2)] = jnp.zeros((rows, wide), BF16)
    at = pl.multiple_of(place[0] * wide, wide)
    for i, b in enumerate((f3, r3)):
        columns[i] = b[:, pl.ds(at, wide)]


def halves_kernel(f3, r3, first, second, sems):
    half = first.shape[0]
    copies = (
        pltpu.make_async_copy(f3.at[pl.ds(0, half)], first, sems.at[0]),
        pltpu.make_async_copy(r3.at[pl.ds(half, half)], second, sems.at[1]),
    )
    for copy in copies:
        copy.start()
    for copy in copies:
        copy.wait()


def last_kernel(place, first_half, second_half, w_own, w_pair, out, columns):
    lhs = jnp.concatenate([first_half[...], second_half[...]], axis=0)
    cols = w_own.shape[1]
    for w, first in ((w_own, 0), (w_pair, cols)):
        out[:, first : first + cols] = dot32(lhs, w[...]).astype(BF16)
    at = pl.multiple_of(place[0] * (LINES * cols), LINES * cols)
    half = first_half.shape[0]
    columns[:half] = first_half[:, pl.ds(at, LINES * cols)]
    columns[half:] = second_half[:, pl.ds(at, LINES * cols)]


def gradient_terms(of_signals, order, place, line, blocks):
    depth, rows = line.shape[0], line.shape[1] - PAD
    pick = iota((SIX, 2 * RANK), 0) & (RANK - 1)
    pick = (pick + (RANK if of_signals else 0) == iota((SIX, 2 * RANK), 1)).astype(F32).astype(BF16)
    slot = lax.shift_right_logical(iota((SIX, rows), 0), 6)
    lhs = []
    for k in order:
        at = lax.rem(place[0] + (depth - k), depth) if of_signals else k
        spread = dot_features(pick, line[at, :rows])
        ids = line[at, rows : rows + PAD][:1].astype(F32).astype(I32)
        lhs.append(jnp.where(slot == ids, spread, 0.0).astype(BF16))
    values = jnp.concatenate([b[...].reshape(-1, b.shape[-1]) for b in blocks], axis=0)
    total = dot32(jnp.concatenate(lhs, axis=1), values)
    cols = total.shape[1] // LINES
    left, right = total[:, :cols], total[:, cols:]
    first = place[1] == 0
    return jnp.where(first, left, right), jnp.where(first, right, left)


def up_gradient_kernel(order, place, line, cot_line, mine, theirs):
    here, there = gradient_terms(False, order, place, line, [cot_line])
    mine[...] = SCALE * here
    theirs[...] = (SCALE * there).astype(BF16)


def down_gradient_kernel(order, place, line, *refs):
    blocks, (up_mine, up_theirs, mine, pair, *guests) = refs[:-8], refs[-8:]
    here, there = gradient_terms(True, order, place, line, blocks)
    mine[...] = here
    own = JOBS * RANK
    pair[0] = there[:own].astype(BF16)
    pair[1] = up_theirs[:own]
    for i, (kept, sent) in enumerate((guests[:2], guests[2:])):
        rows = slice(own + i * RANK, own + (i + 1) * RANK)
        kept[0], kept[1] = here[rows].astype(BF16), up_mine[rows].astype(BF16)
        sent[0], sent[1] = there[rows].astype(BF16), up_theirs[rows]


def finish_kernel(place, adapted, results, last, out):
    z, x = place[0], place[1]
    depth, cols = results.shape[0], results.shape[2] // LINES

    def add(at_z, piece):
        for side, first in ((x, 0), (1 - x, cols)):
            at = pl.multiple_of((at_z * LINES + side) * cols, cols)
            total = piece[:, first : first + cols].astype(F32) + adapted[:, pl.ds(at, cols)].astype(F32)
            out[:, pl.ds(at, cols)] = total.astype(BF16)

    for k in range(depth):
        add(k, results[k])
    add(lax.rem(z + depth // 2, depth), last[...])


def on_device(handed, lengths, placement, frozen, down, up, cotangent):
    sections = lax.axis_size("section")
    devices = lax.axis_size("dp")
    depth = devices // LINES
    far = depth // 2
    s = lax.axis_index("section")
    d = lax.axis_index("dp")
    place = jnp.stack([lax.shift_right_logical(d, 1), d & (LINES - 1), s]).astype(I32)
    plan = placement.reshape(-1)
    lines = [[k * LINES + i for k in range(depth)] for i in range(LINES)]
    rows, width = handed.shape[1:]
    half = rows // 2
    cols = width // devices
    wide = width // depth
    cot = cotangent[0]

    own = lax.ppermute(handed[0], "section", [(i, (i + 1) % sections) for i in range(sections)])

    def to_line(value):
        return lax.all_to_all(value, "dp", 0, 0, axis_index_groups=lines, tiled=True)

    cot_line = to_line(kernel_call(split_kernel, [((depth, rows, wide), BF16)], [], [cot])[0])

    step = lambda pair: (along_z(pair[0], 1, depth), along_z(pair[1], -1, depth))
    ring_1 = step((own, own))

    to_below, to_above = in_order(
        copy_call(maps_kernel, [(2 * RANK, width)] * 2, 4, [place, plan], [down[0], up[0]]), own
    )
    from_above = section_shift(to_below, -1, sections)
    from_below = section_shift(to_above, 1, sections)
    own_down = down[0].reshape(JOBS * RANK, width)
    own_up = up[0].reshape(JOBS * RANK, width)

    w_own = frozen[0]
    w_pair = across_x(in_order((w_own,), own)[0], devices)

    ring_1 = in_order(ring_1, cot_line)
    ring_2 = step(ring_1)
    (own_,) = in_order((own,), ring_1, cot_line, w_pair)
    adapted, sent = kernel_call(
        rows_kernel,
        [((rows, width), BF16), ((depth, rows + PAD, 2 * RANK), BF16)],
        [place, lengths.reshape(-1), plan],
        [own_, cot, own_down, own_up, from_above, from_below],
    )
    line = to_line(sent)

    ring_2 = in_order(ring_2, sent)
    ring_3 = step(ring_2)
    order = (0, 1, depth - 1, 2, depth - 2, 3, depth - 3)
    done, near_columns = kernel_call(
        functools.partial(base_kernel, 5),
        [((5, rows, wide), BF16)] * 2,
        [place],
        [own, *ring_1, *ring_2, w_own, w_pair],
    )

    ring_3 = in_order(ring_3, near_columns)
    half_f, half_r = copy_call(halves_kernel, [(half, width)] * 2, 2, [], ring_3)
    last = along_z(half_f, 1, depth), along_z(half_r, -1, depth)
    ring_3 = in_order(ring_3, half_f)
    results, next_columns = kernel_call(
        functools.partial(owners_kernel, order, depth),
        [((depth, rows, wide), BF16), ((2, rows, wide), BF16)],
        [place],
        [done, *ring_3, w_own, w_pair],
    )
    (line_,) = in_order((line,), results)
    results = to_line(results)
    terms = ((SIX, cols), F32)
    up_mine, up_theirs = kernel_call(
        functools.partial(up_gradient_kernel, tuple(range(depth))),
        [terms, ((SIX, cols), BF16)],
        [place],
        [line_, cot_line],
    )
    last = in_order(last, up_mine)
    last, far_columns = kernel_call(last_kernel, [((rows, wide), BF16)] * 2, [place], [*last, w_own, w_pair], MOVED)
    result_last = along_z(last, far, depth)
    own_rows = JOBS * RANK
    guest = ((2, RANK, cols), BF16)
    down_mine, pair, next_here, next_there, prev_here, prev_there = kernel_call(
        functools.partial(down_gradient_kernel, order + (far,)),
        [terms, ((2, own_rows, cols), BF16)] + [guest] * 4,
        [place],
        [line, near_columns, next_columns, far_columns, up_mine, up_theirs],
        MOVED,
    )

    def to_host(here, there, by):
        moves = [(i, i + by) for i in range(sections) if 0 <= i + by < sections]
        route = [(i * devices + k, j * devices + (k ^ 1)) for i, j in moves for k in range(devices)]
        return section_shift(here, by, sections), lax.ppermute(there, ("section", "dp"), route)

    from_pair = across_x(pair, devices).astype(F32)
    of_below = sum(v.astype(F32) for v in to_host(next_here, next_there, 1))
    of_above = sum(v.astype(F32) for v in to_host(prev_here, prev_there, -1))
    slots = jnp.arange(JOBS, dtype=I32)[:, None, None]

    def hosted(section, code):
        jobs = lax.dynamic_index_in_dim(placement, section, 0, keepdims=False)
        return jnp.sum(jnp.where(jobs[:, 0] == code, jobs[:, 1], 0))

    slot_below, slot_above = hosted(jnp.maximum(s - 1, 0), 2), hosted(jnp.minimum(s + 1, sections - 1), 0)

    def gathered(mine, i):
        return (
            (mine[:own_rows] + from_pair[i]).reshape(JOBS, RANK, cols)
            + jnp.where(slots == slot_below, of_below[i][None], 0.0)
            + jnp.where(slots == slot_above, of_above[i][None], 0.0)
        )[None]

    (passed,) = kernel_call(
        finish_kernel, [((rows, width), BF16)], [place], [adapted, results, result_last]
    )
    return passed[None], gathered(down_mine, 0), gathered(up_mine, 1)


def solution(mesh):
    in_specs = (
        P("section", "dp", None),
        P("section", "dp", None),
        P(),
        P("section", None, "dp"),
        P("section", None, None, None),
        P("section", None, None, None),
        P("section", "dp", None),
    )
    out_specs = (
        P("section", "dp", None),
        P("section", None, None, "dp"),
        P("section", None, None, "dp"),
    )
    return jax.shard_map(on_device, mesh=mesh, in_specs=in_specs, out_specs=out_specs, check_vma=False)
```

```python
import functools

import jax
import jax.numpy as jnp
from jax import lax
from jax.experimental import pallas as pl
from jax.experimental.pallas import tpu as pltpu
from jax.sharding import PartitionSpec as P

RANK = 64
JOBS = 4
SIX = (JOBS + 2) * RANK
SCALE = 0.5
LINES = 2
PAD = 16
MOVED = 2**20
FEATURES = (((1,), (1,)), ((), ()))
BF16, F32, I32 = jnp.bfloat16, jnp.float32, jnp.int32


def dot32(a, b):
    return jnp.dot(a, b, preferred_element_type=F32)


def dot_features(a, b):
    return lax.dot_general(a, b, FEATURES, preferred_element_type=F32)


def along_z(value, by, depth):
    route = [(z * LINES + x, ((z + by) % depth) * LINES + x) for z in range(depth) for x in range(LINES)]
    return lax.ppermute(value, "dp", route)


def across_x(value, devices):
    return lax.ppermute(value, "dp", [(d, d ^ 1) for d in range(devices)])


def section_shift(value, by, sections):
    route = [(i, i + by) for i in range(sections) if 0 <= i + by < sections]
    return lax.ppermute(value, "section", route)


def hosted_slot(plan, section, code):
    first, slot = section * (2 * JOBS), 0
    for j in range(JOBS):
        slot = slot + jnp.where(plan[first + 2 * j] == code, plan[first + 2 * j + 1], 0)
    return slot


def guest_slots(place, plan):
    s, sections = place[2], plan.shape[0] // (2 * JOBS)
    return (
        hosted_slot(plan, jnp.maximum(s - 1, 0), 2),
        hosted_slot(plan, jnp.minimum(s + 1, sections - 1), 0),
    )


def maps_kernel(place, plan, down, up, to_below, to_above, sems):
    copies = []
    for slot, out in zip(guest_slots(place, plan), (to_below, to_above)):
        for i, maps in enumerate((down, up)):
            copies.append(
                pltpu.make_async_copy(maps.at[slot], out.at[pl.ds(i * RANK, RANK)], sems.at[len(copies)])
            )
    for copy in copies:
        copy.start()
    for copy in copies:
        copy.wait()


def copy_call(kernel, outs, copies, scalars, arrays):
    vmem, smem = pl.BlockSpec(memory_space=pltpu.VMEM), pl.BlockSpec(memory_space=pltpu.SMEM)
    return pl.pallas_call(
        kernel,
        out_shape=tuple(jax.ShapeDtypeStruct(shape, BF16) for shape in outs),
        in_specs=[smem] * len(scalars) + [pl.BlockSpec(memory_space=pl.ANY)] * len(arrays),
        out_specs=tuple(vmem for _ in outs),
        scratch_shapes=[pltpu.SemaphoreType.DMA((copies,))],
        compiler_params=pltpu.CompilerParams(vmem_limit_bytes=40 * 2**20),
        cost_estimate=pl.CostEstimate(flops=1024, bytes_accessed=1024, transcendentals=0),
    )(*scalars, *arrays)


def in_order(values, *others):
    return lax.optimization_barrier((tuple(values), others))[0]


def kernel_call(kernel, outs, scalars, arrays, moved=1024):
    vmem, smem = pl.BlockSpec(memory_space=pltpu.VMEM), pl.BlockSpec(memory_space=pltpu.SMEM)
    return pl.pallas_call(
        kernel,
        out_shape=tuple(jax.ShapeDtypeStruct(shape, dtype) for shape, dtype in outs),
        in_specs=[smem] * len(scalars) + [vmem] * len(arrays),
        out_specs=tuple(vmem for _ in outs),
        compiler_params=pltpu.CompilerParams(vmem_limit_bytes=40 * 2**20),
        cost_estimate=pl.CostEstimate(flops=1024, bytes_accessed=moved, transcendentals=0),
    )(*scalars, *arrays)


def split_kernel(cot_ref, out_ref):
    wide = out_ref.shape[2]
    for k in range(out_ref.shape[0]):
        out_ref[k] = cot_ref[:, k * wide : (k + 1) * wide]


def iota(shape, dim):
    return lax.broadcasted_iota(I32, shape, dim)


def rows_kernel(place, lengths, plan, own_x, cot, own_down, own_up, above, below, adapted, sent):
    rows, width = cot.shape
    first = place[2] * (2 * JOBS)
    which = []
    for j in range(JOBS):
        offset, slot = plan[first + 2 * j], plan[first + 2 * j + 1]
        which.append(jnp.where(offset == 1, slot, jnp.where(offset == 2, JOBS, JOBS + 1)))

    def adapter_of(position):
        found, end = jnp.full(position.shape, which[0], I32), 0
        for j in range(1, JOBS):
            end = end + lengths[j - 1]
            found = jnp.where(position >= end, which[j], found)
        return found

    chosen = adapter_of(iota((rows, SIX), 0)) == lax.shift_right_logical(iota((rows, SIX), 1), 6)
    x = own_x[...]
    guest_down = jnp.concatenate([above[:RANK], below[:RANK]], axis=0)
    guest_up = jnp.concatenate([above[RANK:], below[RANK:]], axis=0)

    def all_six(v, own, guest):
        return jnp.concatenate([dot_features(v, own[...]), dot_features(v, guest)], axis=1)

    codes = jnp.where(chosen, all_six(x, own_down, guest_down), 0.0).astype(BF16)
    signals = jnp.where(chosen, SCALE * all_six(cot[...], own_up, guest_up), 0.0).astype(BF16)
    own = JOBS * RANK
    tile = width // 8
    for t in range(8):
        at = slice(t * tile, (t + 1) * tile)
        total = dot32(codes[:, :own], own_up[:, at]) + dot32(codes[:, own:], guest_up[:, at])
        adapted[:, at] = (SCALE * total).astype(BF16)
    rank, lane = iota((SIX, 2 * RANK), 0) & (RANK - 1), iota((SIX, 2 * RANK), 1)
    to_codes = (rank == lane).astype(F32).astype(BF16)
    to_signals = (rank + RANK == lane).astype(F32).astype(BF16)
    narrow = (dot32(codes, to_codes) + dot32(signals, to_signals)).astype(BF16)
    ids = adapter_of(iota((PAD, rows), 1)).astype(F32).astype(BF16)
    for k in range(sent.shape[0]):
        sent[k, :rows] = narrow
        sent[k, rows:] = ids


def base_kernel(count, place, *refs):
    blocks, (w_own, w_pair, out, columns) = refs[:count], refs[count:]
    rows, cols = blocks[0].shape[0], w_own.shape[1]
    wide = LINES * cols
    lhs = jnp.concatenate([b[...] for b in blocks], axis=0)
    for w, first in ((w_own, 0), (w_pair, cols)):
        result = dot32(lhs, w[...]).astype(BF16)
        for i in range(count):
            out[i, :, first : first + cols] = result[i * rows : (i + 1) * rows]
    at = pl.multiple_of(place[0] * wide, wide)
    for i, b in enumerate(blocks):
        columns[i] = b[:, pl.ds(at, wide)]


def owners_kernel(order, places, place, done, f3, r3, w_own, w_pair, out, columns):
    rows, cols = f3.shape[0], w_own.shape[1]
    wide = LINES * cols
    owner = lambda k: lax.rem(place[0] + (places - k), places)
    for i, k in enumerate(order[: done.shape[0]]):
        out[owner(k)] = done[i]
    lhs = jnp.concatenate([f3[...], r3[...]], axis=0)
    for w, first in ((w_own, 0), (w_pair, cols)):
        result = dot32(lhs, w[...]).astype(BF16)
        for i, k in enumerate(order[done.shape[0] :]):
            out[owner(k), :, first : first + cols] = result[i * rows : (i + 1) * rows]
    out[owner(places // 2)] = jnp.zeros((rows, wide), BF16)
    at = pl.multiple_of(place[0] * wide, wide)
    for i, b in enumerate((f3, r3)):
        columns[i] = b[:, pl.ds(at, wide)]


def halves_kernel(f3, r3, first, second, sems):
    half = first.shape[0]
    copies = (
        pltpu.make_async_copy(f3.at[pl.ds(0, half)], first, sems.at[0]),
        pltpu.make_async_copy(r3.at[pl.ds(half, half)], second, sems.at[1]),
    )
    for copy in copies:
        copy.start()
    for copy in copies:
        copy.wait()


def last_kernel(first_half, second_half, w_own, w_pair, out):
    lhs = jnp.concatenate([first_half[...], second_half[...]], axis=0)
    cols = w_own.shape[1]
    for w, first in ((w_own, 0), (w_pair, cols)):
        out[:, first : first + cols] = dot32(lhs, w[...]).astype(BF16)


def gradient_terms(of_signals, order, place, line, blocks):
    depth, rows = line.shape[0], line.shape[1] - PAD
    pick = iota((SIX, 2 * RANK), 0) & (RANK - 1)
    pick = (pick + (RANK if of_signals else 0) == iota((SIX, 2 * RANK), 1)).astype(F32).astype(BF16)
    slot = lax.shift_right_logical(iota((SIX, rows), 0), 6)
    lhs = []
    for k in order:
        at = lax.rem(place[0] + (depth - k), depth) if of_signals else k
        spread = dot_features(pick, line[at, :rows])
        ids = line[at, rows : rows + PAD][:1].astype(F32).astype(I32)
        lhs.append(jnp.where(slot == ids, spread, 0.0).astype(BF16))
    values = jnp.concatenate([b[...].reshape(-1, b.shape[-1]) for b in blocks], axis=0)
    total = dot32(jnp.concatenate(lhs, axis=1), values)
    cols = total.shape[1] // LINES
    left, right = total[:, :cols], total[:, cols:]
    first = place[1] == 0
    return jnp.where(first, left, right), jnp.where(first, right, left)


def up_gradient_kernel(order, place, line, cot_line, mine, theirs):
    here, there = gradient_terms(False, order, place, line, [cot_line])
    mine[...] = SCALE * here
    theirs[...] = (SCALE * there).astype(BF16)


def down_gradient_kernel(order, place, line, *refs):
    blocks, (up_mine, up_theirs, mine, pair, *guests) = refs[:-8], refs[-8:]
    near, next_, *halves = blocks
    wide = near.shape[-1]
    at = pl.multiple_of(place[0] * wide, wide)
    farthest = jnp.concatenate([half[:, pl.ds(at, wide)] for half in halves], axis=0)
    here, there = gradient_terms(True, order, place, line, [near, next_, farthest])
    mine[...] = here
    own = JOBS * RANK
    pair[0] = there[:own].astype(BF16)
    pair[1] = up_theirs[:own]
    for i, (kept, sent) in enumerate((guests[:2], guests[2:])):
        rows = slice(own + i * RANK, own + (i + 1) * RANK)
        kept[0], kept[1] = here[rows].astype(BF16), up_mine[rows].astype(BF16)
        sent[0], sent[1] = there[rows].astype(BF16), up_theirs[rows]


def finish_kernel(place, adapted, results, last, out):
    z, x = place[0], place[1]
    depth, cols = results.shape[0], results.shape[2] // LINES

    def add(at_z, piece):
        for side, first in ((x, 0), (1 - x, cols)):
            at = pl.multiple_of((at_z * LINES + side) * cols, cols)
            total = piece[:, first : first + cols].astype(F32) + adapted[:, pl.ds(at, cols)].astype(F32)
            out[:, pl.ds(at, cols)] = total.astype(BF16)

    for k in range(depth):
        add(k, results[k])
    add(lax.rem(z + depth // 2, depth), last[...])


def on_device(handed, lengths, placement, frozen, down, up, cotangent):
    sections = lax.axis_size("section")
    devices = lax.axis_size("dp")
    depth = devices // LINES
    far = depth // 2
    s = lax.axis_index("section")
    d = lax.axis_index("dp")
    place = jnp.stack([lax.shift_right_logical(d, 1), d & (LINES - 1), s]).astype(I32)
    plan = placement.reshape(-1)
    lines = [[k * LINES + i for k in range(depth)] for i in range(LINES)]
    rows, width = handed.shape[1:]
    half = rows // 2
    cols = width // devices
    wide = width // depth
    cot = cotangent[0]

    own = lax.ppermute(handed[0], "section", [(i, (i + 1) % sections) for i in range(sections)])

    def to_line(value):
        return lax.all_to_all(value, "dp", 0, 0, axis_index_groups=lines, tiled=True)

    cot_line = to_line(kernel_call(split_kernel, [((depth, rows, wide), BF16)], [], [cot])[0])

    step = lambda pair: (along_z(pair[0], 1, depth), along_z(pair[1], -1, depth))
    ring_1 = step((own, own))

    to_below, to_above = in_order(
        copy_call(maps_kernel, [(2 * RANK, width)] * 2, 4, [place, plan], [down[0], up[0]]), own
    )
    from_above = section_shift(to_below, -1, sections)
    from_below = section_shift(to_above, 1, sections)
    own_down = down[0].reshape(JOBS * RANK, width)
    own_up = up[0].reshape(JOBS * RANK, width)

    w_own = frozen[0]
    w_pair = across_x(in_order((w_own,), own)[0], devices)

    ring_1 = in_order(ring_1, cot_line)
    ring_2 = step(ring_1)
    (own_,) = in_order((own,), ring_1, cot_line, w_pair)
    adapted, sent = kernel_call(
        rows_kernel,
        [((rows, width), BF16), ((depth, rows + PAD, 2 * RANK), BF16)],
        [place, lengths.reshape(-1), plan],
        [own_, cot, own_down, own_up, from_above, from_below],
    )
    line = to_line(sent)

    ring_2 = in_order(ring_2, sent)
    ring_3 = step(ring_2)
    order = (0, 1, depth - 1, 2, depth - 2, 3, depth - 3)
    done, near_columns = kernel_call(
        functools.partial(base_kernel, 5),
        [((5, rows, wide), BF16)] * 2,
        [place],
        [own, *ring_1, *ring_2, w_own, w_pair],
    )

    ring_3 = in_order(ring_3, near_columns)
    half_f, half_r = copy_call(halves_kernel, [(half, width)] * 2, 2, [], ring_3)
    last = along_z(half_f, 1, depth), along_z(half_r, -1, depth)
    ring_3 = in_order(ring_3, half_f)
    results, next_columns = kernel_call(
        functools.partial(owners_kernel, order, depth),
        [((depth, rows, wide), BF16), ((2, rows, wide), BF16)],
        [place],
        [done, *ring_3, w_own, w_pair],
    )
    (line_,) = in_order((line,), results)
    results = to_line(results)
    terms = ((SIX, cols), F32)
    up_mine, up_theirs = kernel_call(
        functools.partial(up_gradient_kernel, tuple(range(depth))),
        [terms, ((SIX, cols), BF16)],
        [place],
        [line_, cot_line],
    )
    last = in_order(last, up_mine)
    (last_piece,) = kernel_call(last_kernel, [((rows, wide), BF16)], [], [*last, w_own, w_pair], MOVED)
    result_last = along_z(last_piece, far, depth)
    own_rows = JOBS * RANK
    guest = ((2, RANK, cols), BF16)
    down_mine, pair, next_here, next_there, prev_here, prev_there = kernel_call(
        functools.partial(down_gradient_kernel, order + (far,)),
        [terms, ((2, own_rows, cols), BF16)] + [guest] * 4,
        [place],
        [line, near_columns, next_columns, *last, up_mine, up_theirs],
        MOVED,
    )

    def to_host(here, there, by):
        moves = [(i, i + by) for i in range(sections) if 0 <= i + by < sections]
        route = [(i * devices + k, j * devices + (k ^ 1)) for i, j in moves for k in range(devices)]
        return section_shift(here, by, sections), lax.ppermute(there, ("section", "dp"), route)

    from_pair = across_x(pair, devices).astype(F32)
    of_below = sum(v.astype(F32) for v in to_host(next_here, next_there, 1))
    of_above = sum(v.astype(F32) for v in to_host(prev_here, prev_there, -1))
    slots = jnp.arange(JOBS, dtype=I32)[:, None, None]

    def hosted(section, code):
        jobs = lax.dynamic_index_in_dim(placement, section, 0, keepdims=False)
        return jnp.sum(jnp.where(jobs[:, 0] == code, jobs[:, 1], 0))

    slot_below, slot_above = hosted(jnp.maximum(s - 1, 0), 2), hosted(jnp.minimum(s + 1, sections - 1), 0)

    def gathered(mine, i):
        return (
            (mine[:own_rows] + from_pair[i]).reshape(JOBS, RANK, cols)
            + jnp.where(slots == slot_below, of_below[i][None], 0.0)
            + jnp.where(slots == slot_above, of_above[i][None], 0.0)
        )[None]

    (passed,) = kernel_call(
        finish_kernel, [((rows, width), BF16)], [place], [adapted, results, result_last]
    )
    return passed[None], gathered(down_mine, 0), gathered(up_mine, 1)


def solution(mesh):
    in_specs = (
        P("section", "dp", None),
        P("section", "dp", None),
        P(),
        P("section", None, "dp"),
        P("section", None, None, None),
        P("section", None, None, None),
        P("section", "dp", None),
    )
    out_specs = (
        P("section", "dp", None),
        P("section", None, None, "dp"),
        P("section", None, None, "dp"),
    )
    return jax.shard_map(on_device, mesh=mesh, in_specs=in_specs, out_specs=out_specs, check_vma=False)
```

```python
import functools

import jax
import jax.numpy as jnp
from jax import lax
from jax.experimental import pallas as pl
from jax.experimental.pallas import tpu as pltpu
from jax.sharding import PartitionSpec as P

RANK = 64
JOBS = 4
SIX = (JOBS + 2) * RANK
SCALE = 0.5
LINES = 2
PAD = 16
MOVED = 2**20
FEATURES = (((1,), (1,)), ((), ()))
BF16, F32, I32 = jnp.bfloat16, jnp.float32, jnp.int32


def dot32(a, b):
    return jnp.dot(a, b, preferred_element_type=F32)


def dot_features(a, b):
    return lax.dot_general(a, b, FEATURES, preferred_element_type=F32)


def along_z(value, by, depth):
    route = [(z * LINES + x, ((z + by) % depth) * LINES + x) for z in range(depth) for x in range(LINES)]
    return lax.ppermute(value, "dp", route)


def across_x(value, devices):
    return lax.ppermute(value, "dp", [(d, d ^ 1) for d in range(devices)])


def section_shift(value, by, sections):
    route = [(i, i + by) for i in range(sections) if 0 <= i + by < sections]
    return lax.ppermute(value, "section", route)


def hosted_slot(plan, section, code):
    first, slot = section * (2 * JOBS), 0
    for j in range(JOBS):
        slot = slot + jnp.where(plan[first + 2 * j] == code, plan[first + 2 * j + 1], 0)
    return slot


def guest_slots(place, plan):
    s, sections = place[2], plan.shape[0] // (2 * JOBS)
    return (
        hosted_slot(plan, jnp.maximum(s - 1, 0), 2),
        hosted_slot(plan, jnp.minimum(s + 1, sections - 1), 0),
    )


def maps_kernel(place, plan, down, up, to_below, to_above, sems):
    copies = []
    for slot, out in zip(guest_slots(place, plan), (to_below, to_above)):
        for i, maps in enumerate((down, up)):
            copies.append(
                pltpu.make_async_copy(maps.at[slot], out.at[pl.ds(i * RANK, RANK)], sems.at[len(copies)])
            )
    for copy in copies:
        copy.start()
    for copy in copies:
        copy.wait()


def copy_call(kernel, outs, copies, scalars, arrays):
    vmem, smem = pl.BlockSpec(memory_space=pltpu.VMEM), pl.BlockSpec(memory_space=pltpu.SMEM)
    return pl.pallas_call(
        kernel,
        out_shape=tuple(jax.ShapeDtypeStruct(shape, BF16) for shape in outs),
        in_specs=[smem] * len(scalars) + [pl.BlockSpec(memory_space=pl.ANY)] * len(arrays),
        out_specs=tuple(vmem for _ in outs),
        scratch_shapes=[pltpu.SemaphoreType.DMA((copies,))],
        compiler_params=pltpu.CompilerParams(vmem_limit_bytes=40 * 2**20),
        cost_estimate=pl.CostEstimate(flops=1024, bytes_accessed=1024, transcendentals=0),
    )(*scalars, *arrays)


def in_order(values, *others):
    return lax.optimization_barrier((tuple(values), others))[0]


def kernel_call(kernel, outs, scalars, arrays, moved=1024):
    vmem, smem = pl.BlockSpec(memory_space=pltpu.VMEM), pl.BlockSpec(memory_space=pltpu.SMEM)
    return pl.pallas_call(
        kernel,
        out_shape=tuple(jax.ShapeDtypeStruct(shape, dtype) for shape, dtype in outs),
        in_specs=[smem] * len(scalars) + [vmem] * len(arrays),
        out_specs=tuple(vmem for _ in outs),
        compiler_params=pltpu.CompilerParams(vmem_limit_bytes=40 * 2**20),
        cost_estimate=pl.CostEstimate(flops=1024, bytes_accessed=moved, transcendentals=0),
    )(*scalars, *arrays)


def split_kernel(cot_ref, out_ref):
    wide = out_ref.shape[2]
    for k in range(out_ref.shape[0]):
        out_ref[k] = cot_ref[:, k * wide : (k + 1) * wide]


def iota(shape, dim):
    return lax.broadcasted_iota(I32, shape, dim)


def rows_kernel(place, lengths, plan, own_x, cot, own_down, own_up, above, below, adapted, sent):
    rows, width = cot.shape
    first = place[2] * (2 * JOBS)
    which = []
    for j in range(JOBS):
        offset, slot = plan[first + 2 * j], plan[first + 2 * j + 1]
        which.append(jnp.where(offset == 1, slot, jnp.where(offset == 2, JOBS, JOBS + 1)))

    def adapter_of(position):
        found, end = jnp.full(position.shape, which[0], I32), 0
        for j in range(1, JOBS):
            end = end + lengths[j - 1]
            found = jnp.where(position >= end, which[j], found)
        return found

    chosen = adapter_of(iota((rows, SIX), 0)) == lax.shift_right_logical(iota((rows, SIX), 1), 6)
    x = own_x[...]
    guest_down = jnp.concatenate([above[:RANK], below[:RANK]], axis=0)
    guest_up = jnp.concatenate([above[RANK:], below[RANK:]], axis=0)

    def all_six(v, own, guest):
        return jnp.concatenate([dot_features(v, own[...]), dot_features(v, guest)], axis=1)

    codes = jnp.where(chosen, all_six(x, own_down, guest_down), 0.0).astype(BF16)
    signals = jnp.where(chosen, SCALE * all_six(cot[...], own_up, guest_up), 0.0).astype(BF16)
    own = JOBS * RANK
    tile = width // 8
    for t in range(8):
        at = slice(t * tile, (t + 1) * tile)
        total = dot32(codes[:, :own], own_up[:, at]) + dot32(codes[:, own:], guest_up[:, at])
        adapted[:, at] = (SCALE * total).astype(BF16)
    rank, lane = iota((SIX, 2 * RANK), 0) & (RANK - 1), iota((SIX, 2 * RANK), 1)
    to_codes = (rank == lane).astype(F32).astype(BF16)
    to_signals = (rank + RANK == lane).astype(F32).astype(BF16)
    narrow = (dot32(codes, to_codes) + dot32(signals, to_signals)).astype(BF16)
    ids = adapter_of(iota((PAD, rows), 1)).astype(F32).astype(BF16)
    for k in range(sent.shape[0]):
        sent[k, :rows] = narrow
        sent[k, rows:] = ids


def base_kernel(count, place, *refs):
    blocks, (w_own, w_pair, out, columns) = refs[:count], refs[count:]
    rows, cols = blocks[0].shape[0], w_own.shape[1]
    wide = LINES * cols
    lhs = jnp.concatenate([b[...] for b in blocks], axis=0)
    for w, first in ((w_own, 0), (w_pair, cols)):
        result = dot32(lhs, w[...]).astype(BF16)
        for i in range(count):
            out[i, :, first : first + cols] = result[i * rows : (i + 1) * rows]
    at = pl.multiple_of(place[0] * wide, wide)
    for i, b in enumerate(blocks):
        columns[i] = b[:, pl.ds(at, wide)]


def owners_kernel(order, places, place, done, f3, r3, w_own, w_pair, out, columns):
    rows, cols = f3.shape[0], w_own.shape[1]
    wide = LINES * cols
    owner = lambda k: lax.rem(place[0] + (places - k), places)
    for i, k in enumerate(order[: done.shape[0]]):
        out[owner(k)] = done[i]
    lhs = jnp.concatenate([f3[...], r3[...]], axis=0)
    for w, first in ((w_own, 0), (w_pair, cols)):
        result = dot32(lhs, w[...]).astype(BF16)
        for i, k in enumerate(order[done.shape[0] :]):
            out[owner(k), :, first : first + cols] = result[i * rows : (i + 1) * rows]
    out[owner(places // 2)] = jnp.zeros((rows, wide), BF16)
    at = pl.multiple_of(place[0] * wide, wide)
    for i, b in enumerate((f3, r3)):
        columns[i] = b[:, pl.ds(at, wide)]


def halves_kernel(f3, r3, first, second, sems):
    half = first.shape[0]
    copies = (
        pltpu.make_async_copy(f3.at[pl.ds(0, half)], first, sems.at[0]),
        pltpu.make_async_copy(r3.at[pl.ds(half, half)], second, sems.at[1]),
    )
    for copy in copies:
        copy.start()
    for copy in copies:
        copy.wait()


def last_kernel(place, first_half, second_half, w_own, w_pair, out, columns):
    lhs = jnp.concatenate([first_half[...], second_half[...]], axis=0)
    cols = w_own.shape[1]
    for w, first in ((w_own, 0), (w_pair, cols)):
        out[:, first : first + cols] = dot32(lhs, w[...]).astype(BF16)
    at = pl.multiple_of(place[0] * (LINES * cols), LINES * cols)
    half = first_half.shape[0]
    columns[:half] = first_half[:, pl.ds(at, LINES * cols)]
    columns[half:] = second_half[:, pl.ds(at, LINES * cols)]


def gradient_terms(of_signals, order, place, line, blocks):
    depth, rows = line.shape[0], line.shape[1] - PAD
    pick = iota((SIX, 2 * RANK), 0) & (RANK - 1)
    pick = (pick + (RANK if of_signals else 0) == iota((SIX, 2 * RANK), 1)).astype(F32).astype(BF16)
    slot = lax.shift_right_logical(iota((SIX, rows), 0), 6)
    lhs = []
    for k in order:
        at = lax.rem(place[0] + (depth - k), depth) if of_signals else k
        spread = dot_features(pick, line[at, :rows])
        ids = line[at, rows : rows + PAD][:1].astype(F32).astype(I32)
        lhs.append(jnp.where(slot == ids, spread, 0.0).astype(BF16))
    values = jnp.concatenate([b[...].reshape(-1, b.shape[-1]) for b in blocks], axis=0)
    total = dot32(jnp.concatenate(lhs, axis=1), values)
    cols = total.shape[1] // LINES
    left, right = total[:, :cols], total[:, cols:]
    first = place[1] == 0
    return jnp.where(first, left, right), jnp.where(first, right, left)


def up_gradient_kernel(order, place, line, cot_line, mine, theirs):
    here, there = gradient_terms(False, order, place, line, [cot_line])
    mine[...] = SCALE * here
    theirs[...] = (SCALE * there).astype(BF16)


def down_gradient_kernel(order, place, line, *refs):
    blocks, (up_mine, up_theirs, mine, pair, *guests) = refs[:-8], refs[-8:]
    here, there = gradient_terms(True, order, place, line, blocks)
    mine[...] = here
    own = JOBS * RANK
    pair[0] = there[:own].astype(BF16)
    pair[1] = up_theirs[:own]
    for i, (kept, sent) in enumerate((guests[:2], guests[2:])):
        rows = slice(own + i * RANK, own + (i + 1) * RANK)
        kept[0], kept[1] = here[rows].astype(BF16), up_mine[rows].astype(BF16)
        sent[0], sent[1] = there[rows].astype(BF16), up_theirs[rows]


def finish_kernel(place, adapted, results, last, out):
    z, x = place[0], place[1]
    depth, cols = results.shape[0], results.shape[2] // LINES

    def add(at_z, piece):
        for side, first in ((x, 0), (1 - x, cols)):
            at = pl.multiple_of((at_z * LINES + side) * cols, cols)
            total = piece[:, first : first + cols].astype(F32) + adapted[:, pl.ds(at, cols)].astype(F32)
            out[:, pl.ds(at, cols)] = total.astype(BF16)

    for k in range(depth):
        add(k, results[k])
    add(lax.rem(z + depth // 2, depth), last[...])


def on_device(handed, lengths, placement, frozen, down, up, cotangent):
    sections = lax.axis_size("section")
    devices = lax.axis_size("dp")
    depth = devices // LINES
    far = depth // 2
    s = lax.axis_index("section")
    d = lax.axis_index("dp")
    place = jnp.stack([lax.shift_right_logical(d, 1), d & (LINES - 1), s]).astype(I32)
    plan = placement.reshape(-1)
    lines = [[k * LINES + i for k in range(depth)] for i in range(LINES)]
    rows, width = handed.shape[1:]
    half = rows // 2
    cols = width // devices
    wide = width // depth
    cot = cotangent[0]

    own = lax.ppermute(handed[0], "section", [(i, (i + 1) % sections) for i in range(sections)])

    def to_line(value):
        return lax.all_to_all(value, "dp", 0, 0, axis_index_groups=lines, tiled=True)

    cot_line = to_line(kernel_call(split_kernel, [((depth, rows, wide), BF16)], [], [cot])[0])

    step = lambda pair: (along_z(pair[0], 1, depth), along_z(pair[1], -1, depth))
    ring_1 = step((own, own))

    to_below, to_above = in_order(
        copy_call(maps_kernel, [(2 * RANK, width)] * 2, 4, [place, plan], [down[0], up[0]]), own
    )
    from_above = section_shift(to_below, -1, sections)
    from_below = section_shift(to_above, 1, sections)
    own_down = down[0].reshape(JOBS * RANK, width)
    own_up = up[0].reshape(JOBS * RANK, width)

    w_own = frozen[0]
    w_pair = across_x(in_order((w_own,), to_below)[0], devices)

    ring_1 = in_order(ring_1, cot_line)
    ring_2 = step(ring_1)
    (own_,) = in_order((own,), ring_1, cot_line, w_pair)
    adapted, sent = kernel_call(
        rows_kernel,
        [((rows, width), BF16), ((depth, rows + PAD, 2 * RANK), BF16)],
        [place, lengths.reshape(-1), plan],
        [own_, cot, own_down, own_up, from_above, from_below],
    )
    line = to_line(sent)

    ring_2 = in_order(ring_2, sent)
    ring_3 = step(ring_2)
    order = (0, 1, depth - 1, 2, depth - 2, 3, depth - 3)
    done, near_columns = kernel_call(
        functools.partial(base_kernel, 5),
        [((5, rows, wide), BF16)] * 2,
        [place],
        [own, *ring_1, *ring_2, w_own, w_pair],
    )

    ring_3 = in_order(ring_3, near_columns)
    half_f, half_r = copy_call(halves_kernel, [(half, width)] * 2, 2, [], ring_3)
    last = along_z(half_f, 1, depth), along_z(half_r, -1, depth)
    ring_3 = in_order(ring_3, half_f)
    results, next_columns = kernel_call(
        functools.partial(owners_kernel, order, depth),
        [((depth, rows, wide), BF16), ((2, rows, wide), BF16)],
        [place],
        [done, *ring_3, w_own, w_pair],
    )
    (line_,) = in_order((line,), results)
    results = to_line(results)
    terms = ((SIX, cols), F32)
    up_mine, up_theirs = kernel_call(
        functools.partial(up_gradient_kernel, tuple(range(depth))),
        [terms, ((SIX, cols), BF16)],
        [place],
        [line_, cot_line],
    )
    last = in_order(last, up_mine)
    last, far_columns = kernel_call(last_kernel, [((rows, wide), BF16)] * 2, [place], [*last, w_own, w_pair], MOVED)
    result_last = along_z(last, far, depth)
    own_rows = JOBS * RANK
    guest = ((2, RANK, cols), BF16)
    down_mine, pair, next_here, next_there, prev_here, prev_there = kernel_call(
        functools.partial(down_gradient_kernel, order + (far,)),
        [terms, ((2, own_rows, cols), BF16)] + [guest] * 4,
        [place],
        [line, near_columns, next_columns, far_columns, up_mine, up_theirs],
        MOVED,
    )

    def to_host(here, there, by):
        moves = [(i, i + by) for i in range(sections) if 0 <= i + by < sections]
        route = [(i * devices + k, j * devices + (k ^ 1)) for i, j in moves for k in range(devices)]
        return section_shift(here, by, sections), lax.ppermute(there, ("section", "dp"), route)

    from_pair = across_x(pair, devices).astype(F32)
    of_below = sum(v.astype(F32) for v in to_host(next_here, next_there, 1))
    of_above = sum(v.astype(F32) for v in to_host(prev_here, prev_there, -1))
    slots = jnp.arange(JOBS, dtype=I32)[:, None, None]

    def hosted(section, code):
        jobs = lax.dynamic_index_in_dim(placement, section, 0, keepdims=False)
        return jnp.sum(jnp.where(jobs[:, 0] == code, jobs[:, 1], 0))

    slot_below, slot_above = hosted(jnp.maximum(s - 1, 0), 2), hosted(jnp.minimum(s + 1, sections - 1), 0)

    def gathered(mine, i):
        return (
            (mine[:own_rows] + from_pair[i]).reshape(JOBS, RANK, cols)
            + jnp.where(slots == slot_below, of_below[i][None], 0.0)
            + jnp.where(slots == slot_above, of_above[i][None], 0.0)
        )[None]

    (passed,) = kernel_call(
        finish_kernel, [((rows, width), BF16)], [place], [adapted, results, result_last]
    )
    return passed[None], gathered(down_mine, 0), gathered(up_mine, 1)


def solution(mesh):
    in_specs = (
        P("section", "dp", None),
        P("section", "dp", None),
        P(),
        P("section", None, "dp"),
        P("section", None, None, None),
        P("section", None, None, None),
        P("section", "dp", None),
    )
    out_specs = (
        P("section", "dp", None),
        P("section", None, None, "dp"),
        P("section", None, None, "dp"),
    )
    return jax.shard_map(on_device, mesh=mesh, in_specs=in_specs, out_specs=out_specs, check_vma=False)
```
